512 devices in a mesh: tile: 256 (over z, y, x), filt: 2 (over core).
Axes of the slice: x: 4, y: 8, z: 8, core: 2. Of those that a mesh axis runs over, the one named last changes fastest.
Arguments:
- coarse: bfloat16 [256, 8, 16, 320], P('tile', None, None, 'filt'), may hold values from -6 to 6
- up_weight: bfloat16 [256, 20480], P('filt'), may hold values from -0.125 to 0.125
- up_bias: bfloat16 [256], P('filt'), may hold values from -3 to 3
- mix_weight: bfloat16 [27, 256, 256], P(None, 'filt'), may hold values from -0.078125 to 0.078125
- mix_bias: bfloat16 [256], P('filt'), may hold values from -3 to 3
Outputs:
- fine: bfloat16 [512, 16, 32, 256], P('tile', None, None, 'filt')
The draws below stay inside these ranges and needn't reach their ends.
All inputs are finite; a program needn't handle non-finite values.
Results may differ from the reference program's by a relative error of at most 0.0045.
Values may be sent and summed in bfloat16 or wider, within the bound.
A program may use at most 64 MiB of HBM per device.

```python
import jax
import jax.numpy as jnp
from jax import lax

CIN = 320
CH = 256
XLOW = 16
ZLOW = 8
YLOW = 256


def levels(rng, extent, split, low, top_value):
    gain, own = 1.0, jax.random.fold_in(rng, 6)
    for position, shards_of in split:
        draws = jnp.exp(jax.random.uniform(jax.random.fold_in(own, position), (shards_of,), jnp.float32, low / len(split), top_value / len(split)))
        gain = gain * jnp.repeat(draws, extent[position] // shards_of).reshape([-1 if axis == position else 1 for axis in range(len(extent))])
    return gain


def normal_values(stream_key, extent, width, bound, pieces=(), kind=jnp.bfloat16):
    values = width * jax.random.normal(stream_key, extent, jnp.float32)
    if pieces:
        values = values * levels(stream_key, extent, pieces, -0.22, 0.18)
    return jnp.clip(values, -bound, bound).astype(kind)


def setup_inputs(seed: int = 0) -> dict:
    streams_of = jax.random.split(jax.random.key(seed), 6)
    coarse = normal_values(streams_of[0], (YLOW, ZLOW, XLOW, CIN), 1.0, 6.0, ((0, 256), (3, 2)))
    up_weight = normal_values(streams_of[1], (CH, 64 * CIN), (8 * CIN) ** -0.5, 0.125, ((0, 2),))
    up_bias = normal_values(streams_of[2], (CH,), 0.5, 3.0, ((0, 2),))
    mix_weight = normal_values(streams_of[3], (27, CH, CH), (27 * CH) ** -0.5, 0.078125, ((1, 2),))
    mix_bias = normal_values(streams_of[4], (CH,), 0.5, 3.0, ((0, 2),))
    return dict(coarse=coarse, up_weight=up_weight, up_bias=up_bias, mix_weight=mix_weight, mix_bias=mix_bias)


def reference(coarse, up_weight, up_bias, mix_weight, mix_bias):
    numbers = ("NDHWC", "DHWIO", "NDHWC")
    coarse_std = jnp.transpose(coarse, (0, 2, 1, 3))
    up_std = jnp.transpose(up_weight.reshape(CH, 4, 4, 4, CIN), (1, 2, 3, 4, 0))
    mix_std = jnp.transpose(mix_weight.reshape(3, 3, 3, CH, CH), (0, 1, 2, 4, 3))
    flipped = up_std[::-1, ::-1, ::-1].astype(jnp.float32)
    upsampled = lax.conv_general_dilated(coarse_std[None].astype(jnp.float32), flipped, (1, 1, 1), ((2, 2), (2, 2), (2, 2)), lhs_dilation=(2, 2, 2), dimension_numbers=numbers, preferred_element_type=jnp.float32)[0]
    hidden = (upsampled + up_bias.astype(jnp.float32)).astype(jnp.bfloat16)
    mixed = lax.conv_general_dilated(hidden[None].astype(jnp.float32), mix_std.astype(jnp.float32), (1, 1, 1), ((1, 1), (1, 1), (1, 1)), dimension_numbers=numbers, preferred_element_type=jnp.float32)[0]
    mixed = mixed + mix_bias.astype(jnp.float32)
    result = jnp.maximum(mixed, 0.0).astype(jnp.bfloat16)
    return jnp.transpose(result, (0, 2, 1, 3))
```

```python
import jax
import jax.numpy as jnp
from jax import lax
from jax.experimental import pallas as pl
from jax.experimental.pallas import tpu as pltpu
from jax.sharding import PartitionSpec as P

MESH = pl.DeviceIdType.MESH
NT = (((1,), (1,)), ((), ()))

TAPS = (((-1, 3), (0, 1)), ((0, 2), (1, 0)))


def dot_nt(a, b):
    return lax.dot_general(a, b, NT, preferred_element_type=jnp.float32)


def kernel(
    coarse, upw, upb, mixw, mixb, out,
    cbuf, wup, wmix, ub, mb, xb, hid, scr,
    up_sem, mix_sem, bias_sem, own_sem, send_sem, recv_sem, hsend, hrecv,
):
    tiles = lax.axis_size("tile")
    t = lax.axis_index("tile")
    c = lax.axis_index("filt")
    other = 1 - c
    right = lax.rem(t + 1, tiles)
    left = lax.rem(t + tiles - 1, tiles)
    zl, xl, cs = coarse.shape[1:]
    f = upw.shape[0]
    cin = 2 * cs
    targets = ((t, other), (right, c), (right, other), (left, c), (left, other))
    slots = (1, 0, 0, 2, 2)

    barrier = pltpu.get_barrier_semaphore()
    for dev in targets:
        pl.semaphore_signal(barrier, inc=1, device_id=dev, device_id_type=MESH)

    own_copy = pltpu.make_async_copy(coarse.at[0], cbuf.at[1, c], own_sem)
    own_copy.start()
    bias_copies = [
        pltpu.make_async_copy(upb, ub, bias_sem.at[0]),
        pltpu.make_async_copy(mixb, mb, bias_sem.at[1]),
    ]
    for copy in bias_copies:
        copy.start()
    up_copies = {}
    for px in (0, 1):
        for _, kx in TAPS[px]:
            for ky in range(4):
                cols = pl.ds((16 * ky + 4 * kx) * cin, 4 * cin)
                copy = pltpu.make_async_copy(
                    upw.at[:, cols], wup.at[:, cols], up_sem.at[4 * ky + kx]
                )
                copy.start()
                up_copies[ky, kx] = copy
    mix_copies = []
    for half, src in ((0, c), (1, other)):
        copy = pltpu.make_async_copy(
            mixw.at[:, :, pl.ds(pl.multiple_of(src * f, f), f)], wmix.at[half], mix_sem.at[half]
        )
        copy.start()
        mix_copies.append(copy)

    xb[:, :, :, 0] = jnp.zeros_like(xb[:, :, :, 0])
    xb[:, :, :, zl + 1] = jnp.zeros_like(xb[:, :, :, zl + 1])
    hid[:, :, 0] = jnp.zeros_like(hid[:, :, 0])
    hid[:, :, 2 * zl + 1] = jnp.zeros_like(hid[:, :, 2 * zl + 1])

    pl.semaphore_wait(barrier, 5)
    sends = []
    for k, (dev, slot) in enumerate(zip(targets, slots)):
        copy = pltpu.make_async_remote_copy(
            src_ref=coarse.at[0],
            dst_ref=cbuf.at[slot, c],
            send_sem=send_sem.at[k],
            recv_sem=recv_sem.at[k],
            device_id=dev,
            device_id_type=MESH,
        )
        copy.start()
        sends.append(copy)

    first = (t > 0).astype(jnp.float32)
    last = (t < tiles - 1).astype(jnp.float32)

    def place(slot, scale):
        x = cbuf[slot].astype(jnp.float32)
        x = jnp.concatenate([x[0], x[1]], axis=-1)
        if scale is not None:
            x = x * scale
        gap = jnp.zeros((zl, xl, 64), jnp.float32)
        edge = jnp.zeros((zl, 1, cin + 64), jnp.float32)
        for v, parts in enumerate(([gap, x], [x, gap])):
            y = jnp.concatenate(parts, axis=-1)
            low = jnp.concatenate([edge, y[:, :-1]], axis=1)
            high = jnp.concatenate([y[:, 1:], edge], axis=1)
            for s, w in enumerate((low, y, high)):
                xb[v, s, slot, 1 : zl + 1] = w.astype(jnp.bfloat16)

    own_copy.wait()
    sends[0].wait_recv()
    place(1, None)
    sends[1].wait_recv()
    sends[2].wait_recv()
    place(0, first)
    sends[3].wait_recv()
    sends[4].wait_recv()
    place(2, last)

    for copy in bias_copies:
        copy.wait()
    ubias = ub[...].astype(jnp.float32).reshape(1, 1, 1, f)
    mbias = mb[...].astype(jnp.float32).reshape(1, f)

    m = 2 * zl * xl
    swaps = []
    for px in (0, 1):
        for _, kx in TAPS[px]:
            for ky in range(4):
                up_copies[ky, kx].wait()
        for pz in (0, 1):
            lhs, even, odd = [], [], []
            for yt in (0, 1):
                for dz, kz in TAPS[pz]:
                    for dx, kx in TAPS[px]:
                        lhs.append(
                            xb[pz, dx + 1, yt : yt + 2, dz + 1 : dz + 1 + zl].reshape(m, cin + 64)
                        )
                        for ky, group in ((2 - 2 * yt, even), (3 - 2 * yt, odd)):
                            start = (16 * ky + 4 * kx + kz) * cin - (0 if pz else 64)
                            group.append(wup[:, start : start + cin + 64])
            rhs = jnp.concatenate(
                [jnp.concatenate(even, axis=1), jnp.concatenate(odd, axis=1)], axis=0
            )
            up = dot_nt(jnp.concatenate(lhs, axis=1), rhs)
            for q in (0, 1):
                for j in (0, 1):
                    r = 2 * j + q
                    h = up[j * zl * xl : (j + 1) * zl * xl, q * f : (q + 1) * f]
                    h = h.reshape(zl, xl, f) + ubias[0]
                    if r == 0:
                        h = h * first
                    if r == 3:
                        h = h * last
                    edge = jnp.zeros((zl, 1, f), jnp.float32)
                    if px:
                        moved = jnp.concatenate([edge, h[:, :-1]], axis=1)
                    else:
                        moved = jnp.concatenate([h[:, 1:], edge], axis=1)
                    h = h.astype(jnp.bfloat16)
                    moved = moved.astype(jnp.bfloat16)
                    for i in range(zl):
                        zz = 1 + 2 * i + pz
                        hid[0, r, zz, :, (1 + px) * f : (2 + px) * f] = h[i]
                        lane = 0 if px else 3 * f
                        hid[0, r, zz, :, lane : lane + f] = moved[i]
        copy = pltpu.make_async_remote_copy(
            src_ref=hid.at[0, :, pl.ds(1, 2 * zl), :, pl.ds((1 + px) * f, f)],
            dst_ref=hid.at[1, :, pl.ds(1, 2 * zl), :, pl.ds((1 + px) * f, f)],
            send_sem=hsend.at[px],
            recv_sem=hrecv.at[px],
            device_id=(t, other),
            device_id_type=MESH,
        )
        copy.start()
        swaps.append(copy)

    def mix(half):
        lhs = [[], []]
        groups = [[], []]
        blank = jnp.zeros((f, 3 * f), jnp.bfloat16)
        for r in range(4):
            for dz in range(3):
                for p in (0, 1):
                    lhs[p].append(
                        hid[half, r, dz : dz + 2 * zl, :, p * f : (p + 3) * f].reshape(m, 3 * f)
                    )
                for a in (0, 1):
                    dy = r - a
                    if 0 <= dy < 3:
                        taps = [wmix[half, 9 * dy + 3 * dx + dz] for dx in range(3)]
                        groups[a].append(jnp.concatenate(taps, axis=1))
                    else:
                        groups[a].append(blank)
        rhs = jnp.concatenate([jnp.concatenate(g, axis=1) for g in groups], axis=0)
        left_side = jnp.concatenate([jnp.concatenate(g, axis=1) for g in lhs], axis=0)
        return dot_nt(left_side, rhs)

    mix_copies[0].wait()
    total = mix(0)
    for copy in swaps:
        copy.wait_recv()
    for px in (0, 1):
        for r in range(4):
            h = hid[1, r, 1 : 2 * zl + 1, :, (1 + px) * f : (2 + px) * f].astype(jnp.float32)
            edge = jnp.zeros((2 * zl, 1, f), jnp.float32)
            if px:
                moved = jnp.concatenate([edge, h[:, :-1]], axis=1)
            else:
                moved = jnp.concatenate([h[:, 1:], edge], axis=1)
            lane = 0 if px else 3 * f
            hid[1, r, 1 : 2 * zl + 1, :, lane : lane + f] = moved.astype(jnp.bfloat16)
    mix_copies[1].wait()
    total = total + mix(1)

    for a in (0, 1):
        for p in (0, 1):
            y = total[p * m : (p + 1) * m, a * f : (a + 1) * f] + mbias
            y = jnp.maximum(y, 0.0).reshape(2 * zl, xl, f)
            scr[:, pl.ds(p, xl, stride=2), :] = y
        out[a] = scr[...].astype(jnp.bfloat16)

    for copy in sends:
        copy.wait_send()
    for copy in swaps:
        copy.wait_send()


def local(coarse, up_weight, up_bias, mix_weight, mix_bias):
    _, zl, xl, cs = coarse.shape
    f = up_weight.shape[0]
    bf16 = jnp.bfloat16
    anywhere = pl.BlockSpec(memory_space=pl.ANY)
    return pl.pallas_call(
        kernel,
        out_shape=jax.ShapeDtypeStruct((2, 2 * zl, 2 * xl, f), bf16),
        in_specs=[anywhere] * 5,
        out_specs=pl.BlockSpec(memory_space=pltpu.VMEM),
        scratch_shapes=[
            pltpu.VMEM((3, 2, zl, xl, cs), bf16),
            pltpu.VMEM(up_weight.shape, bf16),
            pltpu.VMEM((2, 27, f, f), bf16),
            pltpu.VMEM((f,), bf16),
            pltpu.VMEM((f,), bf16),
            pltpu.VMEM((2, 3, 3, zl + 2, xl, 2 * cs + 64), bf16),
            pltpu.VMEM((2, 4, 2 * zl + 2, xl, 4 * f), bf16),
            pltpu.VMEM((2 * zl, 2 * xl, f), jnp.float32),
            pltpu.SemaphoreType.DMA((16,)),
            pltpu.SemaphoreType.DMA((2,)),
            pltpu.SemaphoreType.DMA((2,)),
            pltpu.SemaphoreType.DMA,
            pltpu.SemaphoreType.DMA((5,)),
            pltpu.SemaphoreType.DMA((5,)),
            pltpu.SemaphoreType.DMA((2,)),
            pltpu.SemaphoreType.DMA((2,)),
        ],
        compiler_params=pltpu.CompilerParams(
            collective_id=0, has_side_effects=True, vmem_limit_bytes=60 * 1024 * 1024
        ),
        cost_estimate=pl.CostEstimate(
            flops=2_500_000_000, bytes_accessed=8_000_000, transcendentals=0
        ),
        name="section",
    )(coarse, up_weight, up_bias, mix_weight, mix_bias)


def solution(mesh):
    placed = (
        P("tile", None, None, "filt"),
        P("filt", None),
        P("filt"),
        P(None, "filt", None),
        P("filt"),
    )
    return jax.shard_map(
        local, mesh=mesh, in_specs=placed, out_specs=P("tile", None, None, "filt"), check_vma=False
    )
```

```python
import jax
import jax.numpy as jnp
from jax import lax
from jax.experimental import pallas as pl
from jax.experimental.pallas import tpu as pltpu
from jax.sharding import PartitionSpec as P

MESH = pl.DeviceIdType.MESH
NT = (((1,), (1,)), ((), ()))

TAPS = (((-1, 3), (0, 1)), ((0, 2), (1, 0)))


def dot_nt(a, b):
    return lax.dot_general(a, b, NT, preferred_element_type=jnp.float32)


def kernel(
    coarse, upw, upb, mixw, mixb, out,
    cbuf, wup, wmix, ub, mb, xb, hid, scr,
    up_sem, mix_sem, bias_sem, own_sem, send_sem, recv_sem, hsend, hrecv,
):
    tiles = lax.axis_size("tile")
    t = lax.axis_index("tile")
    c = lax.axis_index("filt")
    other = 1 - c
    right = t + 1
    left = t - 1
    zl, xl, cs = coarse.shape[1:]
    f = upw.shape[0]
    cin = 2 * cs
    targets = ((t, other), (right, c), (right, other), (left, c), (left, other))
    slots = (1, 0, 0, 2, 2)

    has_left = t > 0
    has_right = t < tiles - 1

    def each(action):
        action(0)

        @pl.when(has_right)
        def _():
            action(1)
            action(2)

        @pl.when(has_left)
        def _():
            action(3)
            action(4)

    barrier = pltpu.get_barrier_semaphore()
    each(
        lambda k: pl.semaphore_signal(
            barrier, inc=1, device_id=targets[k], device_id_type=MESH
        )
    )

    own_copy = pltpu.make_async_copy(coarse.at[0], cbuf.at[1, c], own_sem)
    own_copy.start()
    bias_copies = [
        pltpu.make_async_copy(upb, ub, bias_sem.at[0]),
        pltpu.make_async_copy(mixb, mb, bias_sem.at[1]),
    ]
    for copy in bias_copies:
        copy.start()
    up_copies = {}
    for px in (0, 1):
        for _, kx in TAPS[px]:
            for ky in range(4):
                cols = pl.ds((16 * ky + 4 * kx) * cin, 4 * cin)
                copy = pltpu.make_async_copy(
                    upw.at[:, cols], wup.at[:, cols], up_sem.at[4 * ky + kx]
                )
                copy.start()
                up_copies[ky, kx] = copy
    mix_copies = []
    for half, src in ((0, c), (1, other)):
        copy = pltpu.make_async_copy(
            mixw.at[:, :, pl.ds(pl.multiple_of(src * f, f), f)], wmix.at[half], mix_sem.at[half]
        )
        copy.start()
        mix_copies.append(copy)

    xb[:, :, :, 0] = jnp.zeros_like(xb[:, :, :, 0])
    xb[:, :, :, zl + 1] = jnp.zeros_like(xb[:, :, :, zl + 1])
    hid[:, :, 0] = jnp.zeros_like(hid[:, :, 0])
    hid[:, :, 2 * zl + 1] = jnp.zeros_like(hid[:, :, 2 * zl + 1])

    @pl.when(jnp.logical_not(has_left))
    def _():
        cbuf[0] = jnp.zeros_like(cbuf[0])

    @pl.when(jnp.logical_not(has_right))
    def _():
        cbuf[2] = jnp.zeros_like(cbuf[2])

    first = has_left.astype(jnp.int32)
    last = has_right.astype(jnp.int32)
    pl.semaphore_wait(barrier, 1 + 2 * first + 2 * last)
    sends = [
        pltpu.make_async_remote_copy(
            src_ref=coarse.at[0],
            dst_ref=cbuf.at[slot, c],
            send_sem=send_sem.at[k],
            recv_sem=recv_sem.at[k],
            device_id=dev,
            device_id_type=MESH,
        )
        for k, (dev, slot) in enumerate(zip(targets, slots))
    ]
    each(lambda k: sends[k].start())
    first = first.astype(jnp.float32)
    last = last.astype(jnp.float32)

    def place(slot):
        x = cbuf[slot].astype(jnp.float32)
        x = jnp.concatenate([x[0], x[1]], axis=-1)
        gap = jnp.zeros((zl, xl, 64), jnp.float32)
        edge = jnp.zeros((zl, 1, cin + 64), jnp.float32)
        for v, parts in enumerate(([gap, x], [x, gap])):
            y = jnp.concatenate(parts, axis=-1)
            low = jnp.concatenate([edge, y[:, :-1]], axis=1)
            high = jnp.concatenate([y[:, 1:], edge], axis=1)
            for s, w in enumerate((low, y, high)):
                xb[v, s, slot, 1 : zl + 1] = w.astype(jnp.bfloat16)

    own_copy.wait()
    sends[0].wait_recv()
    place(1)

    @pl.when(has_left)
    def _():
        sends[1].wait_recv()
        sends[2].wait_recv()

    place(0)

    @pl.when(has_right)
    def _():
        sends[3].wait_recv()
        sends[4].wait_recv()

    place(2)

    for copy in bias_copies:
        copy.wait()
    ubias = ub[...].astype(jnp.float32).reshape(1, 1, 1, f)
    mbias = mb[...].astype(jnp.float32).reshape(1, f)

    m = 2 * zl * xl
    swaps = []
    for px in (0, 1):
        for _, kx in TAPS[px]:
            for ky in range(4):
                up_copies[ky, kx].wait()
        for pz in (0, 1):
            lhs, even, odd = [], [], []
            for yt in (0, 1):
                for dz, kz in TAPS[pz]:
                    for dx, kx in TAPS[px]:
                        lhs.append(
                            xb[pz, dx + 1, yt : yt + 2, dz + 1 : dz + 1 + zl].reshape(m, cin + 64)
                        )
                        for ky, group in ((2 - 2 * yt, even), (3 - 2 * yt, odd)):
                            start = (16 * ky + 4 * kx + kz) * cin - (0 if pz else 64)
                            group.append(wup[:, start : start + cin + 64])
            rhs = jnp.concatenate(
                [jnp.concatenate(even, axis=1), jnp.concatenate(odd, axis=1)], axis=0
            )
            up = dot_nt(jnp.concatenate(lhs, axis=1), rhs)
            for q in (0, 1):
                for j in (0, 1):
                    r = 2 * j + q
                    h = up[j * zl * xl : (j + 1) * zl * xl, q * f : (q + 1) * f]
                    h = h.reshape(zl, xl, f) + ubias[0]
                    if r == 0:
                        h = h * first
                    if r == 3:
                        h = h * last
                    edge = jnp.zeros((zl, 1, f), jnp.float32)
                    if px:
                        moved = jnp.concatenate([edge, h[:, :-1]], axis=1)
                    else:
                        moved = jnp.concatenate([h[:, 1:], edge], axis=1)
                    h = h.astype(jnp.bfloat16)
                    moved = moved.astype(jnp.bfloat16)
                    for i in range(zl):
                        zz = 1 + 2 * i + pz
                        hid[0, r, zz, :, (1 + px) * f : (2 + px) * f] = h[i]
                        lane = 0 if px else 3 * f
                        hid[0, r, zz, :, lane : lane + f] = moved[i]
        copy = pltpu.make_async_remote_copy(
            src_ref=hid.at[0, :, pl.ds(1, 2 * zl), :, pl.ds((1 + px) * f, f)],
            dst_ref=hid.at[1, :, pl.ds(1, 2 * zl), :, pl.ds((1 + px) * f, f)],
            send_sem=hsend.at[px],
            recv_sem=hrecv.at[px],
            device_id=(t, other),
            device_id_type=MESH,
        )
        copy.start()
        swaps.append(copy)

    def mix(half):
        lhs = [[], []]
        groups = [[], []]
        blank = jnp.zeros((f, 3 * f), jnp.bfloat16)
        for r in range(4):
            for dz in range(3):
                for p in (0, 1):
                    lhs[p].append(
                        hid[half, r, dz : dz + 2 * zl, :, p * f : (p + 3) * f].reshape(m, 3 * f)
                    )
                for a in (0, 1):
                    dy = r - a
                    if 0 <= dy < 3:
                        taps = [wmix[half, 9 * dy + 3 * dx + dz] for dx in range(3)]
                        groups[a].append(jnp.concatenate(taps, axis=1))
                    else:
                        groups[a].append(blank)
        rhs = jnp.concatenate([jnp.concatenate(g, axis=1) for g in groups], axis=0)
        left_side = jnp.concatenate([jnp.concatenate(g, axis=1) for g in lhs], axis=0)
        return dot_nt(left_side, rhs)

    mix_copies[0].wait()
    total = mix(0)
    for copy in swaps:
        copy.wait_recv()
    for px in (0, 1):
        for r in range(4):
            h = hid[1, r, 1 : 2 * zl + 1, :, (1 + px) * f : (2 + px) * f].astype(jnp.float32)
            edge = jnp.zeros((2 * zl, 1, f), jnp.float32)
            if px:
                moved = jnp.concatenate([edge, h[:, :-1]], axis=1)
            else:
                moved = jnp.concatenate([h[:, 1:], edge], axis=1)
            lane = 0 if px else 3 * f
            hid[1, r, 1 : 2 * zl + 1, :, lane : lane + f] = moved.astype(jnp.bfloat16)
    mix_copies[1].wait()
    total = total + mix(1)

    for a in (0, 1):
        for p in (0, 1):
            y = total[p * m : (p + 1) * m, a * f : (a + 1) * f] + mbias
            y = jnp.maximum(y, 0.0).reshape(2 * zl, xl, f)
            scr[:, pl.ds(p, xl, stride=2), :] = y
        out[a] = scr[...].astype(jnp.bfloat16)

    each(lambda k: sends[k].wait_send())
    for copy in swaps:
        copy.wait_send()


def local(coarse, up_weight, up_bias, mix_weight, mix_bias):
    _, zl, xl, cs = coarse.shape
    f = up_weight.shape[0]
    bf16 = jnp.bfloat16
    anywhere = pl.BlockSpec(memory_space=pl.ANY)
    return pl.pallas_call(
        kernel,
        out_shape=pltpu.VMEM((2, 2 * zl, 2 * xl, f), bf16),
        in_specs=[pl.BlockSpec(memory_space=pltpu.HBM)] * 5,
        out_specs=pl.BlockSpec(memory_space=pltpu.VMEM),
        scratch_shapes=[
            pltpu.VMEM((3, 2, zl, xl, cs), bf16),
            pltpu.VMEM(up_weight.shape, bf16),
            pltpu.VMEM((2, 27, f, f), bf16),
            pltpu.VMEM((f,), bf16),
            pltpu.VMEM((f,), bf16),
            pltpu.VMEM((2, 3, 3, zl + 2, xl, 2 * cs + 64), bf16),
            pltpu.VMEM((2, 4, 2 * zl + 2, xl, 4 * f), bf16),
            pltpu.VMEM((2 * zl, 2 * xl, f), jnp.float32),
            pltpu.SemaphoreType.DMA((16,)),
            pltpu.SemaphoreType.DMA((2,)),
            pltpu.SemaphoreType.DMA((2,)),
            pltpu.SemaphoreType.DMA,
            pltpu.SemaphoreType.DMA((5,)),
            pltpu.SemaphoreType.DMA((5,)),
            pltpu.SemaphoreType.DMA((2,)),
            pltpu.SemaphoreType.DMA((2,)),
        ],
        compiler_params=pltpu.CompilerParams(
            collective_id=0, has_side_effects=True, vmem_limit_bytes=62 * 1024 * 1024
        ),
        cost_estimate=pl.CostEstimate(
            flops=2_500_000_000, bytes_accessed=8_000_000, transcendentals=0
        ),
        name="section",
    )(coarse, up_weight, up_bias, mix_weight, mix_bias)


def solution(mesh):
    placed = (
        P("tile", None, None, "filt"),
        P("filt", None),
        P("filt"),
        P(None, "filt", None),
        P("filt"),
    )
    return jax.shard_map(
        local, mesh=mesh, in_specs=placed, out_specs=P("tile", None, None, "filt"), check_vma=False
    )
```

```python
import jax
import jax.numpy as jnp
from jax import lax
from jax.experimental import pallas as pl
from jax.experimental.pallas import tpu as pltpu
from jax.sharding import PartitionSpec as P

MESH = pl.DeviceIdType.MESH
NT = (((1,), (1,)), ((), ()))

TAPS = (((-1, 3), (0, 1)), ((0, 2), (1, 0)))


def dot_nt(a, b):
    return lax.dot_general(a, b, NT, preferred_element_type=jnp.float32)


def kernel(
    coarse, upw, upb, mixw, mixb, out,
    own, cmain, ctail, wup, wmix, ub, mb, xb, hid, scr,
    up_sem, mix_sem, bias_sem, own_sem, send_sem, recv_sem, hsend, hrecv,
):
    tiles = lax.axis_size("tile")
    t = lax.axis_index("tile")
    c = lax.axis_index("filt")
    other = 1 - c
    right = t + 1
    left = t - 1
    zl, xl, cs = coarse.shape[1:]
    f = upw.shape[0]
    cin = 2 * cs
    targets = ((t, other), (right, c), (right, other), (left, c), (left, other))
    slots = (1, 0, 0, 2, 2)

    has_left = t > 0
    has_right = t < tiles - 1

    def each(action):
        action(0)

        @pl.when(has_right)
        def _():
            action(1)
            action(2)

        @pl.when(has_left)
        def _():
            action(3)
            action(4)

    barrier = pltpu.get_barrier_semaphore()
    each(
        lambda k: pl.semaphore_signal(
            barrier, inc=1, device_id=targets[k], device_id_type=MESH
        )
    )

    own_copies = [
        pltpu.make_async_copy(coarse.at[0], own, own_sem.at[0]),
        pltpu.make_async_copy(coarse.at[0, :, :, 0:128], cmain.at[1, c], own_sem.at[1]),
    ]
    for copy in own_copies:
        copy.start()
    bias_copies = [
        pltpu.make_async_copy(upb, ub, bias_sem.at[0]),
        pltpu.make_async_copy(mixb, mb, bias_sem.at[1]),
    ]
    for copy in bias_copies:
        copy.start()
    up_copies = {}
    for px in (0, 1):
        for _, kx in TAPS[px]:
            for ky in range(4):
                cols = pl.ds((16 * ky + 4 * kx) * cin, 4 * cin)
                copy = pltpu.make_async_copy(
                    upw.at[:, cols], wup.at[:, cols], up_sem.at[4 * ky + kx]
                )
                copy.start()
                up_copies[ky, kx] = copy
    mix_copies = []
    for half, src in ((0, c), (1, other)):
        copy = pltpu.make_async_copy(
            mixw.at[:, :, pl.ds(pl.multiple_of(src * f, f), f)], wmix.at[half], mix_sem.at[half]
        )
        copy.start()
        mix_copies.append(copy)

    @pl.when(jnp.logical_not(has_left))
    def _():
        cmain[0] = jnp.zeros_like(cmain[0])
        ctail[0] = jnp.zeros_like(ctail[0])

    @pl.when(jnp.logical_not(has_right))
    def _():
        cmain[2] = jnp.zeros_like(cmain[2])
        ctail[2] = jnp.zeros_like(ctail[2])

    first = has_left.astype(jnp.int32)
    last = has_right.astype(jnp.int32)
    pl.semaphore_wait(barrier, 1 + 2 * first + 2 * last)
    sends = [
        [
            pltpu.make_async_remote_copy(
                src_ref=src,
                dst_ref=dst,
                send_sem=send_sem.at[part, k],
                recv_sem=recv_sem.at[part, k],
                device_id=dev,
                device_id_type=MESH,
            )
            for part, (src, dst) in enumerate(
                (
                    (coarse.at[0, :, :, 0:128], cmain.at[slot, c]),
                    (ctail.at[1, c], ctail.at[slot, c]),
                )
            )
        ]
        for k, (dev, slot) in enumerate(zip(targets, slots))
    ]
    each(lambda k: sends[k][0].start())
    own_copies[0].wait()
    tail = own[:, :, 128:cs].astype(jnp.float32)
    for i in range(zl // 4):
        ctail[1, c, i] = jnp.concatenate(
            [tail[4 * i + j] for j in range(4)], axis=-1
        ).astype(jnp.bfloat16)
    each(lambda k: sends[k][1].start())

    xb[:, :, :, 0] = jnp.zeros_like(xb[:, :, :, 0])
    xb[:, :, :, zl + 1] = jnp.zeros_like(xb[:, :, :, zl + 1])
    hid[:, :, 0] = jnp.zeros_like(hid[:, :, 0])
    hid[:, :, 2 * zl + 1] = jnp.zeros_like(hid[:, :, 2 * zl + 1])
    first = first.astype(jnp.float32)
    last = last.astype(jnp.float32)

    def place(slot):
        parts = []
        for half in (0, 1):
            parts.append(cmain[slot, half].astype(jnp.float32))
            packed = ctail[slot, half].astype(jnp.float32)
            tails = [
                packed[z // 4, :, (z % 4) * 32 : (z % 4) * 32 + 32] for z in range(zl)
            ]
            parts.append(jnp.stack(tails, axis=0))
        x = jnp.concatenate(parts, axis=-1)
        gap = jnp.zeros((zl, xl, 64), jnp.float32)
        edge = jnp.zeros((zl, 1, cin + 64), jnp.float32)
        for v, parts in enumerate(([gap, x], [x, gap])):
            y = jnp.concatenate(parts, axis=-1)
            low = jnp.concatenate([edge, y[:, :-1]], axis=1)
            high = jnp.concatenate([y[:, 1:], edge], axis=1)
            for s, w in enumerate((low, y, high)):
                xb[v, s, slot, 1 : zl + 1] = w.astype(jnp.bfloat16)

    def arrived(*which):
        for k in which:
            sends[k][0].wait_recv()
            sends[k][1].wait_recv()

    own_copies[1].wait()
    arrived(0)
    place(1)

    for copy in (*bias_copies, *up_copies.values(), *mix_copies):
        copy.wait()
    ubias = ub[...].astype(jnp.float32).reshape(1, 1, 1, f)
    mbias = mb[...].astype(jnp.float32).reshape(1, f)

    @pl.when(has_left)
    def _():
        arrived(1, 2)

    @pl.when(has_right)
    def _():
        arrived(3, 4)

    place(0)
    place(2)

    m = 2 * zl * xl
    swaps = []
    for px in (0, 1):
        for pz in (0, 1):
            lhs, even, odd = [], [], []
            for yt in (0, 1):
                for dz, kz in TAPS[pz]:
                    for dx, kx in TAPS[px]:
                        lhs.append(
                            xb[pz, dx + 1, yt : yt + 2, dz + 1 : dz + 1 + zl].reshape(m, cin + 64)
                        )
                        for ky, group in ((2 - 2 * yt, even), (3 - 2 * yt, odd)):
                            start = (16 * ky + 4 * kx + kz) * cin - (0 if pz else 64)
                            group.append(wup[:, start : start + cin + 64])
            rhs = jnp.concatenate(
                [jnp.concatenate(even, axis=1), jnp.concatenate(odd, axis=1)], axis=0
            )
            up = dot_nt(jnp.concatenate(lhs, axis=1), rhs)
            for q in (0, 1):
                for j in (0, 1):
                    r = 2 * j + q
                    h = up[j * zl * xl : (j + 1) * zl * xl, q * f : (q + 1) * f]
                    h = h.reshape(zl, xl, f) + ubias[0]
                    if r == 0:
                        h = h * first
                    if r == 3:
                        h = h * last
                    edge = jnp.zeros((zl, 1, f), jnp.float32)
                    if px:
                        moved = jnp.concatenate([edge, h[:, :-1]], axis=1)
                    else:
                        moved = jnp.concatenate([h[:, 1:], edge], axis=1)
                    h = h.astype(jnp.bfloat16)
                    moved = moved.astype(jnp.bfloat16)
                    for i in range(zl):
                        zz = 1 + 2 * i + pz
                        hid[0, r, zz, :, (1 + px) * f : (2 + px) * f] = h[i]
                        lane = 0 if px else 3 * f
                        hid[0, r, zz, :, lane : lane + f] = moved[i]
        copy = pltpu.make_async_remote_copy(
            src_ref=hid.at[0, :, pl.ds(1, 2 * zl), :, pl.ds((1 + px) * f, f)],
            dst_ref=hid.at[1, :, pl.ds(1, 2 * zl), :, pl.ds((1 + px) * f, f)],
            send_sem=hsend.at[px],
            recv_sem=hrecv.at[px],
            device_id=(t, other),
            device_id_type=MESH,
        )
        copy.start()
        swaps.append(copy)

    def mix(half):
        lhs = [[], []]
        groups = [[], []]
        blank = jnp.zeros((f, 3 * f), jnp.bfloat16)
        for r in range(4):
            for dz in range(3):
                for p in (0, 1):
                    lhs[p].append(
                        hid[half, r, dz : dz + 2 * zl, :, p * f : (p + 3) * f].reshape(m, 3 * f)
                    )
                for a in (0, 1):
                    dy = r - a
                    if 0 <= dy < 3:
                        taps = [wmix[half, 9 * dy + 3 * dx + dz] for dx in range(3)]
                        groups[a].append(jnp.concatenate(taps, axis=1))
                    else:
                        groups[a].append(blank)
        rhs = jnp.concatenate([jnp.concatenate(g, axis=1) for g in groups], axis=0)
        left_side = jnp.concatenate([jnp.concatenate(g, axis=1) for g in lhs], axis=0)
        return dot_nt(left_side, rhs)

    total = mix(0)
    for copy in swaps:
        copy.wait_recv()
    for px in (0, 1):
        for r in range(4):
            h = hid[1, r, 1 : 2 * zl + 1, :, (1 + px) * f : (2 + px) * f].astype(jnp.float32)
            edge = jnp.zeros((2 * zl, 1, f), jnp.float32)
            if px:
                moved = jnp.concatenate([edge, h[:, :-1]], axis=1)
            else:
                moved = jnp.concatenate([h[:, 1:], edge], axis=1)
            lane = 0 if px else 3 * f
            hid[1, r, 1 : 2 * zl + 1, :, lane : lane + f] = moved.astype(jnp.bfloat16)
    total = total + mix(1)

    for a in (0, 1):
        for p in (0, 1):
            y = total[p * m : (p + 1) * m, a * f : (a + 1) * f] + mbias
            y = jnp.maximum(y, 0.0).reshape(2 * zl, xl, f)
            scr[:, pl.ds(p, xl, stride=2), :] = y
        out[a] = scr[...].astype(jnp.bfloat16)

    each(lambda k: (sends[k][0].wait_send(), sends[k][1].wait_send()))
    for copy in swaps:
        copy.wait_send()


def local(coarse, up_weight, up_bias, mix_weight, mix_bias):
    _, zl, xl, cs = coarse.shape
    f = up_weight.shape[0]
    bf16 = jnp.bfloat16
    anywhere = pl.BlockSpec(memory_space=pl.ANY)
    return pl.pallas_call(
        kernel,
        out_shape=pltpu.VMEM((2, 2 * zl, 2 * xl, f), bf16),
        in_specs=[pl.BlockSpec(memory_space=pltpu.HBM)] * 5,
        out_specs=pl.BlockSpec(memory_space=pltpu.VMEM),
        scratch_shapes=[
            pltpu.VMEM((zl, xl, cs), bf16),
            pltpu.VMEM((3, 2, zl, xl, 128), bf16),
            pltpu.VMEM((3, 2, zl // 4, xl, 128), bf16),
            pltpu.VMEM(up_weight.shape, bf16),
            pltpu.VMEM((2, 27, f, f), bf16),
            pltpu.VMEM((f,), bf16),
            pltpu.VMEM((f,), bf16),
            pltpu.VMEM((2, 3, 3, zl + 2, xl, 2 * cs + 64), bf16),
            pltpu.VMEM((2, 4, 2 * zl + 2, xl, 4 * f), bf16),
            pltpu.VMEM((2 * zl, 2 * xl, f), jnp.float32),
            pltpu.SemaphoreType.DMA((16,)),
            pltpu.SemaphoreType.DMA((2,)),
            pltpu.SemaphoreType.DMA((2,)),
            pltpu.SemaphoreType.DMA((2,)),
            pltpu.SemaphoreType.DMA((2, 5)),
            pltpu.SemaphoreType.DMA((2, 5)),
            pltpu.SemaphoreType.DMA((2,)),
            pltpu.SemaphoreType.DMA((2,)),
        ],
        compiler_params=pltpu.CompilerParams(
            collective_id=0, has_side_effects=True, vmem_limit_bytes=62 * 1024 * 1024
        ),
        cost_estimate=pl.CostEstimate(
            flops=2_500_000_000, bytes_accessed=8_000_000, transcendentals=0
        ),
        name="section",
    )(coarse, up_weight, up_bias, mix_weight, mix_bias)


def solution(mesh):
    placed = (
        P("tile", None, None, "filt"),
        P("filt", None),
        P("filt"),
        P(None, "filt", None),
        P("filt"),
    )
    return jax.shard_map(
        local, mesh=mesh, in_specs=placed, out_specs=P("tile", None, None, "filt"), check_vma=False
    )
```

```python
import jax
import jax.numpy as jnp
from jax import lax
from jax.experimental import pallas as pl
from jax.experimental.pallas import tpu as pltpu
from jax.sharding import PartitionSpec as P

MESH = pl.DeviceIdType.MESH
NT = (((1,), (1,)), ((), ()))

TAPS = (((-1, 3), (0, 1)), ((0, 2), (1, 0)))


def dot_nt(a, b):
    return lax.dot_general(a, b, NT, preferred_element_type=jnp.float32)


def kernel(
    coarse, upw, upb, mixw, mixb, out,
    own, cmain, ctail, wup, wmix, ub, mb, xb, hid, scr, acc,
    up_sem, mix_sem, bias_sem, own_sem, send_sem, recv_sem, hand_send, hand_recv, hsend, hrecv,
):
    tiles = lax.axis_size("tile")
    t = lax.axis_index("tile")
    c = lax.axis_index("filt")
    other = 1 - c
    right = t + 1
    left = t - 1
    zl, xl, cs = coarse.shape[1:]
    f = upw.shape[0]
    cin = 2 * cs
    targets = ((t, other), (right, c), (right, other), (left, c), (left, other))
    slots = (1, 0, 0, 2, 2)

    has_left = t > 0
    has_right = t < tiles - 1

    corner = jnp.logical_and(t == 0, c == 0)
    hands_on = jnp.logical_and(t == 0, c == 1)

    def each(action, to_right, to_left):
        action(0)

        @pl.when(to_right)
        def _():
            action(1)
            action(2)

        for k, core in ((3, c), (4, other)):

            @pl.when(to_left(core))
            def _(k=k):
                action(k)

    def sends_left(core):
        return jnp.logical_or(t > 1, jnp.logical_and(t == 1, core == 1))

    barrier = pltpu.get_barrier_semaphore()
    each(
        lambda k: pl.semaphore_signal(
            barrier, inc=1, device_id=targets[k], device_id_type=MESH
        ),
        jnp.logical_and(has_right, jnp.logical_not(corner)),
        lambda core: has_left,
    )

    own_copies = [
        pltpu.make_async_copy(coarse.at[0], own, own_sem.at[0]),
        pltpu.make_async_copy(coarse.at[0, :, :, 0:128], cmain.at[1, c], own_sem.at[1]),
    ]
    for copy in own_copies:
        copy.start()
    bias_copies = [
        pltpu.make_async_copy(upb, ub, bias_sem.at[0]),
        pltpu.make_async_copy(mixb, mb, bias_sem.at[1]),
    ]
    for copy in bias_copies:
        copy.start()
    up_copies = {}
    for px in (0, 1):
        for _, kx in TAPS[px]:
            for ky in range(4):
                cols = pl.ds((16 * ky + 4 * kx) * cin, 4 * cin)
                copy = pltpu.make_async_copy(
                    upw.at[:, cols], wup.at[:, cols], up_sem.at[4 * ky + kx]
                )
                copy.start()
                up_copies[ky, kx] = copy
    mix_copies = []
    for half, src in ((0, c), (1, other)):
        copy = pltpu.make_async_copy(
            mixw.at[:, :, pl.ds(pl.multiple_of(src * f, f), f)], wmix.at[half], mix_sem.at[half]
        )
        copy.start()
        mix_copies.append(copy)

    @pl.when(jnp.logical_not(has_left))
    def _():
        cmain[0] = jnp.zeros_like(cmain[0])
        ctail[0] = jnp.zeros_like(ctail[0])

    @pl.when(jnp.logical_not(has_right))
    def _():
        cmain[2] = jnp.zeros_like(cmain[2])
        ctail[2] = jnp.zeros_like(ctail[2])

    first = has_left.astype(jnp.int32)
    last = has_right.astype(jnp.int32)
    pl.semaphore_wait(barrier, 1 + 2 * first + 2 * last - (t == 1).astype(jnp.int32))
    sends = [
        [
            pltpu.make_async_remote_copy(
                src_ref=src,
                dst_ref=dst,
                send_sem=send_sem.at[part, k],
                recv_sem=recv_sem.at[part, k],
                device_id=dev,
                device_id_type=MESH,
            )
            for part, (src, dst) in enumerate(
                (
                    (coarse.at[0, :, :, 0:128], cmain.at[slot, c]),
                    (ctail.at[1, c], ctail.at[slot, c]),
                )
            )
        ]
        for k, (dev, slot) in enumerate(zip(targets, slots))
    ]
    each(lambda k: sends[k][0].start(), has_right, sends_left)
    own_copies[0].wait()
    tail = own[:, :, 128:cs].astype(jnp.float32)
    for i in range(zl // 4):
        ctail[1, c, i] = jnp.concatenate(
            [tail[4 * i + j] for j in range(4)], axis=-1
        ).astype(jnp.bfloat16)
    each(lambda k: sends[k][1].start(), has_right, sends_left)

    handed = [
        pltpu.make_async_remote_copy(
            src_ref=buf.at[2],
            dst_ref=buf.at[2],
            send_sem=hand_send.at[part],
            recv_sem=hand_recv.at[part],
            device_id=(t, other),
            device_id_type=MESH,
        )
        for part, buf in enumerate((cmain, ctail))
    ]

    def arrived(*which):
        for k in which:
            sends[k][0].wait_recv()
            sends[k][1].wait_recv()

    @pl.when(hands_on)
    def _():
        arrived(3, 4)
        for copy in handed:
            copy.start()

    xb[:, :, :, 0] = jnp.zeros_like(xb[:, :, :, 0])
    xb[:, :, :, zl + 1] = jnp.zeros_like(xb[:, :, :, zl + 1])
    hid[:, :, 0] = jnp.zeros_like(hid[:, :, 0])
    hid[:, :, 2 * zl + 1] = jnp.zeros_like(hid[:, :, 2 * zl + 1])
    first = first.astype(jnp.float32)
    last = last.astype(jnp.float32)

    def place(slot):
        parts = []
        for half in (0, 1):
            parts.append(cmain[slot, half].astype(jnp.float32))
            packed = ctail[slot, half].astype(jnp.float32)
            tails = [
                packed[z // 4, :, (z % 4) * 32 : (z % 4) * 32 + 32] for z in range(zl)
            ]
            parts.append(jnp.stack(tails, axis=0))
        x = jnp.concatenate(parts, axis=-1)
        gap = jnp.zeros((zl, xl, 64), jnp.float32)
        edge = jnp.zeros((zl, 1, cin + 64), jnp.float32)
        for v, parts in enumerate(([gap, x], [x, gap])):
            y = jnp.concatenate(parts, axis=-1)
            low = jnp.concatenate([edge, y[:, :-1]], axis=1)
            high = jnp.concatenate([y[:, 1:], edge], axis=1)
            for s, w in enumerate((low, y, high)):
                xb[v, s, slot, 1 : zl + 1] = w.astype(jnp.bfloat16)

    own_copies[1].wait()
    arrived(0)
    place(1)

    for copy in (*bias_copies, *[up_copies[ky, kx] for ky in range(4) for kx in (1, 3)]):
        copy.wait()
    ubias = ub[...].astype(jnp.float32).reshape(1, 1, 1, f)
    mbias = mb[...].astype(jnp.float32).reshape(1, f)

    @pl.when(has_left)
    def _():
        arrived(1, 2)

    @pl.when(jnp.logical_and(has_right, t > 0))
    def _():
        arrived(3, 4)

    @pl.when(corner)
    def _():
        for copy in handed:
            copy.wait_recv()

    place(0)
    place(2)

    m = 2 * zl * xl
    swaps = []
    for px in (0, 1):
        if px:
            for copy in (*[up_copies[ky, kx] for ky in range(4) for kx in (0, 2)], *mix_copies):
                copy.wait()
        for pz in (0, 1):
            lhs, even, odd = [], [], []
            for yt in (0, 1):
                for dz, kz in TAPS[pz]:
                    for dx, kx in TAPS[px]:
                        lhs.append(
                            xb[pz, dx + 1, yt : yt + 2, dz + 1 : dz + 1 + zl].reshape(m, cin + 64)
                        )
                        for ky, group in ((2 - 2 * yt, even), (3 - 2 * yt, odd)):
                            start = (16 * ky + 4 * kx + kz) * cin - (0 if pz else 64)
                            group.append(wup[:, start : start + cin + 64])
            rhs = jnp.concatenate(
                [jnp.concatenate(even, axis=1), jnp.concatenate(odd, axis=1)], axis=0
            )
            up = dot_nt(jnp.concatenate(lhs, axis=1), rhs)
            for q in (0, 1):
                for j in (0, 1):
                    r = 2 * j + q
                    h = up[j * zl * xl : (j + 1) * zl * xl, q * f : (q + 1) * f]
                    h = h.reshape(zl, xl, f) + ubias[0]
                    if r == 0:
                        h = h * first
                    if r == 3:
                        h = h * last
                    edge = jnp.zeros((zl, 1, f), jnp.float32)
                    if px:
                        moved = jnp.concatenate([edge, h[:, :-1]], axis=1)
                    else:
                        moved = jnp.concatenate([h[:, 1:], edge], axis=1)
                    h = h.astype(jnp.bfloat16)
                    moved = moved.astype(jnp.bfloat16)
                    for i in range(zl):
                        zz = 1 + 2 * i + pz
                        hid[0, r, zz, :, (1 + px) * f : (2 + px) * f] = h[i]
                        lane = 0 if px else 3 * f
                        hid[0, r, zz, :, lane : lane + f] = moved[i]
        copy = pltpu.make_async_remote_copy(
            src_ref=hid.at[0, :, pl.ds(1, 2 * zl), :, pl.ds((1 + px) * f, f)],
            dst_ref=hid.at[1, :, pl.ds(1, 2 * zl), :, pl.ds((1 + px) * f, f)],
            send_sem=hsend.at[px],
            recv_sem=hrecv.at[px],
            device_id=(t, other),
            device_id_type=MESH,
        )
        copy.start()
        swaps.append(copy)

    def mix(half):
        lhs = [[], []]
        groups = [[], []]
        blank = jnp.zeros((f, 3 * f), jnp.bfloat16)
        for r in range(4):
            for dz in range(3):
                for p in (0, 1):
                    lhs[p].append(
                        hid[half, r, dz : dz + 2 * zl, :, p * f : (p + 3) * f].reshape(m, 3 * f)
                    )
                for a in (0, 1):
                    dy = r - a
                    if 0 <= dy < 3:
                        taps = [wmix[half, 9 * dy + 3 * dx + dz] for dx in range(3)]
                        groups[a].append(jnp.concatenate(taps, axis=1))
                    else:
                        groups[a].append(blank)
        rhs = jnp.concatenate([jnp.concatenate(g, axis=1) for g in groups], axis=0)
        left_side = jnp.concatenate([jnp.concatenate(g, axis=1) for g in lhs], axis=0)
        return dot_nt(left_side, rhs)

    @pl.when(c >= 0)
    def _():
        acc[...] = mix(0)

    for copy in swaps:
        copy.wait_recv()
    for px in (0, 1):
        for r in range(4):
            h = hid[1, r, 1 : 2 * zl + 1, :, (1 + px) * f : (2 + px) * f].astype(jnp.float32)
            edge = jnp.zeros((2 * zl, 1, f), jnp.float32)
            if px:
                moved = jnp.concatenate([edge, h[:, :-1]], axis=1)
            else:
                moved = jnp.concatenate([h[:, 1:], edge], axis=1)
            lane = 0 if px else 3 * f
            hid[1, r, 1 : 2 * zl + 1, :, lane : lane + f] = moved.astype(jnp.bfloat16)
    total = acc[...] + mix(1)

    for a in (0, 1):
        for p in (0, 1):
            y = total[p * m : (p + 1) * m, a * f : (a + 1) * f] + mbias
            y = jnp.maximum(y, 0.0).reshape(2 * zl, xl, f)
            scr[:, pl.ds(p, xl, stride=2), :] = y
        out[a] = scr[...].astype(jnp.bfloat16)

    each(
        lambda k: (sends[k][0].wait_send(), sends[k][1].wait_send()), has_right, sends_left
    )

    @pl.when(hands_on)
    def _():
        for copy in handed:
            copy.wait_send()

    for copy in swaps:
        copy.wait_send()


def local(coarse, up_weight, up_bias, mix_weight, mix_bias):
    _, zl, xl, cs = coarse.shape
    f = up_weight.shape[0]
    bf16 = jnp.bfloat16
    anywhere = pl.BlockSpec(memory_space=pl.ANY)
    return pl.pallas_call(
        kernel,
        out_shape=pltpu.VMEM((2, 2 * zl, 2 * xl, f), bf16),
        in_specs=[pl.BlockSpec(memory_space=pltpu.HBM)] * 5,
        out_specs=pl.BlockSpec(memory_space=pltpu.VMEM),
        scratch_shapes=[
            pltpu.VMEM((zl, xl, cs), bf16),
            pltpu.VMEM((3, 2, zl, xl, 128), bf16),
            pltpu.VMEM((3, 2, zl // 4, xl, 128), bf16),
            pltpu.VMEM(up_weight.shape, bf16),
            pltpu.VMEM((2, 27, f, f), bf16),
            pltpu.VMEM((f,), bf16),
            pltpu.VMEM((f,), bf16),
            pltpu.VMEM((2, 3, 3, zl + 2, xl, 2 * cs + 64), bf16),
            pltpu.VMEM((2, 4, 2 * zl + 2, xl, 4 * f), bf16),
            pltpu.VMEM((2 * zl, 2 * xl, f), jnp.float32),
            pltpu.VMEM((4 * zl * xl, 2 * f), jnp.float32),
            pltpu.SemaphoreType.DMA((16,)),
            pltpu.SemaphoreType.DMA((2,)),
            pltpu.SemaphoreType.DMA((2,)),
            pltpu.SemaphoreType.DMA((2,)),
            pltpu.SemaphoreType.DMA((2, 5)),
            pltpu.SemaphoreType.DMA((2, 5)),
            pltpu.SemaphoreType.DMA((2,)),
            pltpu.SemaphoreType.DMA((2,)),
            pltpu.SemaphoreType.DMA((2,)),
            pltpu.SemaphoreType.DMA((2,)),
        ],
        compiler_params=pltpu.CompilerParams(
            collective_id=0, has_side_effects=True, vmem_limit_bytes=62 * 1024 * 1024
        ),
        cost_estimate=pl.CostEstimate(
            flops=2_500_000_000, bytes_accessed=8_000_000, transcendentals=0
        ),
        name="section",
    )(coarse, up_weight, up_bias, mix_weight, mix_bias)


def solution(mesh):
    placed = (
        P("tile", None, None, "filt"),
        P("filt", None),
        P("filt"),
        P(None, "filt", None),
        P("filt"),
    )
    return jax.shard_map(
        local, mesh=mesh, in_specs=placed, out_specs=P("tile", None, None, "filt"), check_vma=False
    )
```

```python
import jax
import jax.numpy as jnp
from jax import lax
from jax.experimental import pallas as pl
from jax.experimental.pallas import tpu as pltpu
from jax.sharding import PartitionSpec as P

MESH = pl.DeviceIdType.MESH
NT = (((1,), (1,)), ((), ()))

TAPS = (((-1, 3), (0, 1)), ((0, 2), (1, 0)))


def dot_nt(a, b):
    return lax.dot_general(a, b, NT, preferred_element_type=jnp.float32)


def kernel(
    coarse, upw, upb, mixw, mixb, out,
    own, cmain, ctail, wup, wmix, ub, mb, xb, hid, scr, acc,
    up_sem, mix_sem, bias_sem, own_sem, send_sem, recv_sem, hand_send, hand_recv, hsend, hrecv,
):
    tiles = lax.axis_size("tile")
    t = lax.axis_index("tile")
    c = lax.axis_index("filt")
    other = 1 - c
    right = t + 1
    left = t - 1
    zl, xl, cs = coarse.shape[1:]
    f = upw.shape[0]
    cin = 2 * cs
    targets = ((t, other), (right, c), (right, other), (left, c), (left, other))
    slots = (1, 0, 0, 2, 2)

    has_left = t > 0
    has_right = t < tiles - 1

    corner = jnp.logical_and(t == 0, c == 0)
    hands_on = jnp.logical_and(t == 0, c == 1)

    def each(action, to_right, to_left):
        @pl.when(to_right)
        def _():
            action(1)
            action(2)

        for k, core in ((3, c), (4, other)):

            @pl.when(to_left(core))
            def _(k=k):
                action(k)

        action(0)

    def sends_left(core):
        return jnp.logical_or(t > 1, jnp.logical_and(t == 1, core == 1))

    barrier = pltpu.get_barrier_semaphore()
    each(
        lambda k: pl.semaphore_signal(
            barrier, inc=1, device_id=targets[k], device_id_type=MESH
        ),
        jnp.logical_and(has_right, jnp.logical_not(corner)),
        lambda core: has_left,
    )

    own_copies = [
        pltpu.make_async_copy(coarse.at[0], own, own_sem.at[0]),
        pltpu.make_async_copy(coarse.at[0, :, :, 0:128], cmain.at[1, c], own_sem.at[1]),
    ]
    for copy in own_copies:
        copy.start()
    bias_copies = [
        pltpu.make_async_copy(upb, ub, bias_sem.at[0]),
        pltpu.make_async_copy(mixb, mb, bias_sem.at[1]),
    ]
    up_copies = {}
    for kx in range(4):
        for ky in range(4):
            cols = pl.ds((16 * ky + 4 * kx) * cin, 4 * cin)
            up_copies[ky, kx] = pltpu.make_async_copy(
                upw.at[:, cols], wup.at[:, cols], up_sem.at[4 * ky + kx]
            )
    up_groups = [[up_copies[ky, kx] for _, kx in TAPS[px] for ky in range(4)] for px in (0, 1)]
    mix_copies = [
        pltpu.make_async_copy(
            mixw.at[:, :, pl.ds(pl.multiple_of(src * f, f), f)], wmix.at[half], mix_sem.at[half]
        )
        for half, src in ((0, c), (1, other))
    ]
    for copy in up_groups[0]:
        copy.start()

    @pl.when(jnp.logical_not(has_left))
    def _():
        cmain[0] = jnp.zeros_like(cmain[0])
        ctail[0] = jnp.zeros_like(ctail[0])

    @pl.when(jnp.logical_not(has_right))
    def _():
        cmain[2] = jnp.zeros_like(cmain[2])
        ctail[2] = jnp.zeros_like(ctail[2])

    first = has_left.astype(jnp.int32)
    last = has_right.astype(jnp.int32)
    pl.semaphore_wait(barrier, 1 + 2 * first + 2 * last - (t == 1).astype(jnp.int32))
    sends = [
        [
            pltpu.make_async_remote_copy(
                src_ref=src,
                dst_ref=dst,
                send_sem=send_sem.at[part, k],
                recv_sem=recv_sem.at[part, k],
                device_id=dev,
                device_id_type=MESH,
            )
            for part, (src, dst) in enumerate(
                (
                    (coarse.at[0, :, :, 0:128], cmain.at[slot, c]),
                    (ctail.at[1, c], ctail.at[slot, c]),
                )
            )
        ]
        for k, (dev, slot) in enumerate(zip(targets, slots))
    ]
    each(lambda k: sends[k][0].start(), has_right, sends_left)
    for copy in (*up_groups[1], *mix_copies, *bias_copies):
        copy.start()

    own_copies[0].wait()
    tail = own[:, :, 128:cs].astype(jnp.float32)
    for i in range(zl // 4):
        ctail[1, c, i] = jnp.concatenate(
            [tail[4 * i + j] for j in range(4)], axis=-1
        ).astype(jnp.bfloat16)
    each(lambda k: sends[k][1].start(), has_right, sends_left)

    handed = [
        pltpu.make_async_remote_copy(
            src_ref=buf.at[2],
            dst_ref=buf.at[2],
            send_sem=hand_send.at[part],
            recv_sem=hand_recv.at[part],
            device_id=(t, other),
            device_id_type=MESH,
        )
        for part, buf in enumerate((cmain, ctail))
    ]

    def arrived(*which):
        for k in which:
            sends[k][0].wait_recv()
            sends[k][1].wait_recv()

    @pl.when(hands_on)
    def _():
        arrived(3, 4)
        for copy in handed:
            copy.start()

    xb[:, :, :, 0] = jnp.zeros_like(xb[:, :, :, 0])
    xb[:, :, :, zl + 1] = jnp.zeros_like(xb[:, :, :, zl + 1])
    hid[:, :, 0] = jnp.zeros_like(hid[:, :, 0])
    hid[:, :, 2 * zl + 1] = jnp.zeros_like(hid[:, :, 2 * zl + 1])
    first = first.astype(jnp.float32)
    last = last.astype(jnp.float32)

    def place(slot):
        parts = []
        for half in (0, 1):
            parts.append(cmain[slot, half].astype(jnp.float32))
            packed = ctail[slot, half].astype(jnp.float32)
            tails = [
                packed[z // 4, :, (z % 4) * 32 : (z % 4) * 32 + 32] for z in range(zl)
            ]
            parts.append(jnp.stack(tails, axis=0))
        x = jnp.concatenate(parts, axis=-1)
        gap = jnp.zeros((zl, xl, 64), jnp.float32)
        edge = jnp.zeros((zl, 1, cin + 64), jnp.float32)
        for v, parts in enumerate(([gap, x], [x, gap])):
            y = jnp.concatenate(parts, axis=-1)
            low = jnp.concatenate([edge, y[:, :-1]], axis=1)
            high = jnp.concatenate([y[:, 1:], edge], axis=1)
            for s, w in enumerate((low, y, high)):
                xb[v, s, slot, 1 : zl + 1] = w.astype(jnp.bfloat16)

    own_copies[1].wait()
    arrived(0)
    place(1)

    for copy in (*bias_copies, *[up_copies[ky, kx] for ky in range(4) for kx in (1, 3)]):
        copy.wait()
    ubias = ub[...].astype(jnp.float32).reshape(1, 1, 1, f)
    mbias = mb[...].astype(jnp.float32).reshape(1, f)

    @pl.when(has_left)
    def _():
        arrived(1, 2)

    @pl.when(jnp.logical_and(has_right, t > 0))
    def _():
        arrived(3, 4)

    @pl.when(corner)
    def _():
        for copy in handed:
            copy.wait_recv()

    place(0)
    place(2)

    m = 2 * zl * xl
    swaps = []
    for px in (0, 1):
        if px:
            for copy in (*[up_copies[ky, kx] for ky in range(4) for kx in (0, 2)], *mix_copies):
                copy.wait()
        for pz in (0, 1):
            lhs, even, odd = [], [], []
            for yt in (0, 1):
                for dz, kz in TAPS[pz]:
                    for dx, kx in TAPS[px]:
                        lhs.append(
                            xb[pz, dx + 1, yt : yt + 2, dz + 1 : dz + 1 + zl].reshape(m, cin + 64)
                        )
                        for ky, group in ((2 - 2 * yt, even), (3 - 2 * yt, odd)):
                            start = (16 * ky + 4 * kx + kz) * cin - (0 if pz else 64)
                            group.append(wup[:, start : start + cin + 64])
            rhs = jnp.concatenate(
                [jnp.concatenate(even, axis=1), jnp.concatenate(odd, axis=1)], axis=0
            )
            up = dot_nt(jnp.concatenate(lhs, axis=1), rhs)
            for q in (0, 1):
                for j in (0, 1):
                    r = 2 * j + q
                    h = up[j * zl * xl : (j + 1) * zl * xl, q * f : (q + 1) * f]
                    h = h.reshape(zl, xl, f) + ubias[0]
                    if r == 0:
                        h = h * first
                    if r == 3:
                        h = h * last
                    edge = jnp.zeros((zl, 1, f), jnp.float32)
                    if px:
                        moved = jnp.concatenate([edge, h[:, :-1]], axis=1)
                    else:
                        moved = jnp.concatenate([h[:, 1:], edge], axis=1)
                    h = h.astype(jnp.bfloat16)
                    moved = moved.astype(jnp.bfloat16)
                    for i in range(zl):
                        zz = 1 + 2 * i + pz
                        hid[0, r, zz, :, (1 + px) * f : (2 + px) * f] = h[i]
                        lane = 0 if px else 3 * f
                        hid[0, r, zz, :, lane : lane + f] = moved[i]
        copy = pltpu.make_async_remote_copy(
            src_ref=hid.at[0, :, pl.ds(1, 2 * zl), :, pl.ds((1 + px) * f, f)],
            dst_ref=hid.at[1, :, pl.ds(1, 2 * zl), :, pl.ds((1 + px) * f, f)],
            send_sem=hsend.at[px],
            recv_sem=hrecv.at[px],
            device_id=(t, other),
            device_id_type=MESH,
        )
        copy.start()
        swaps.append(copy)

    def window(half, r, dz, xs):
        lanes = slice(xs[0] * f, (xs[-1] + 1) * f)
        return hid[half, r, dz : dz + 2 * zl, :, lanes].reshape(m, len(xs) * f)

    def tap(half, a, p, r, x, dz):
        dy, dx = r - a, x - p
        if 0 <= dy < 3 and 0 <= dx < 3:
            return wmix[half, 9 * dy + 3 * dx + dz]
        return jnp.zeros((f, f), jnp.bfloat16)

    groups = (
        ((1, 2), (1, 2), ((0, 0), (0, 1), (1, 0), (1, 1))),
        ((0,), (1, 2), ((0, 0), (0, 1))),
        ((3,), (1, 2), ((1, 0), (1, 1))),
        ((0, 1, 2, 3), (0,), ((0, 0), (1, 0))),
        ((0, 1, 2, 3), (3,), ((0, 1), (1, 1))),
    )

    def mix(half):
        parts = {}
        for rows, xs, outs in groups:
            steps = [(r, dz) for r in rows for dz in range(3)]
            lhs = jnp.concatenate([window(half, r, dz, xs) for r, dz in steps], axis=1)
            rhs = jnp.concatenate(
                [
                    jnp.concatenate(
                        [tap(half, a, p, r, x, dz) for r, dz in steps for x in xs], axis=1
                    )
                    for a, p in outs
                ],
                axis=0,
            )
            got = dot_nt(lhs, rhs)
            for i, key in enumerate(outs):
                part = got[:, i * f : (i + 1) * f]
                parts[key] = parts[key] + part if key in parts else part
        return parts

    @pl.when(c >= 0)
    def _():
        for (a, p), part in mix(0).items():
            acc[a, p] = part

    for copy in swaps:
        copy.wait_recv()
    for px in (0, 1):
        for r in range(4):
            h = hid[1, r, 1 : 2 * zl + 1, :, (1 + px) * f : (2 + px) * f].astype(jnp.float32)
            edge = jnp.zeros((2 * zl, 1, f), jnp.float32)
            if px:
                moved = jnp.concatenate([edge, h[:, :-1]], axis=1)
            else:
                moved = jnp.concatenate([h[:, 1:], edge], axis=1)
            lane = 0 if px else 3 * f
            hid[1, r, 1 : 2 * zl + 1, :, lane : lane + f] = moved.astype(jnp.bfloat16)
    rest = mix(1)

    for a in (0, 1):
        for p in (0, 1):
            y = acc[a, p] + rest[a, p] + mbias
            y = jnp.maximum(y, 0.0).reshape(2 * zl, xl, f)
            scr[:, pl.ds(p, xl, stride=2), :] = y
        out[a] = scr[...].astype(jnp.bfloat16)

    each(
        lambda k: (sends[k][0].wait_send(), sends[k][1].wait_send()), has_right, sends_left
    )

    @pl.when(hands_on)
    def _():
        for copy in handed:
            copy.wait_send()

    for copy in swaps:
        copy.wait_send()


def local(coarse, up_weight, up_bias, mix_weight, mix_bias):
    _, zl, xl, cs = coarse.shape
    f = up_weight.shape[0]
    bf16 = jnp.bfloat16
    anywhere = pl.BlockSpec(memory_space=pl.ANY)
    return pl.pallas_call(
        kernel,
        out_shape=pltpu.VMEM((2, 2 * zl, 2 * xl, f), bf16),
        in_specs=[pl.BlockSpec(memory_space=pltpu.HBM)] * 5,
        out_specs=pl.BlockSpec(memory_space=pltpu.VMEM),
        scratch_shapes=[
            pltpu.VMEM((zl, xl, cs), bf16),
            pltpu.VMEM((3, 2, zl, xl, 128), bf16),
            pltpu.VMEM((3, 2, zl // 4, xl, 128), bf16),
            pltpu.VMEM(up_weight.shape, bf16),
            pltpu.VMEM((2, 27, f, f), bf16),
            pltpu.VMEM((f,), bf16),
            pltpu.VMEM((f,), bf16),
            pltpu.VMEM((2, 3, 3, zl + 2, xl, 2 * cs + 64), bf16),
            pltpu.VMEM((2, 4, 2 * zl + 2, xl, 4 * f), bf16),
            pltpu.VMEM((2 * zl, 2 * xl, f), jnp.float32),
            pltpu.VMEM((2, 2, 2 * zl * xl, f), jnp.float32),
            pltpu.SemaphoreType.DMA((16,)),
            pltpu.SemaphoreType.DMA((2,)),
            pltpu.SemaphoreType.DMA((2,)),
            pltpu.SemaphoreType.DMA((2,)),
            pltpu.SemaphoreType.DMA((2, 5)),
            pltpu.SemaphoreType.DMA((2, 5)),
            pltpu.SemaphoreType.DMA((2,)),
            pltpu.SemaphoreType.DMA((2,)),
            pltpu.SemaphoreType.DMA((2,)),
            pltpu.SemaphoreType.DMA((2,)),
        ],
        compiler_params=pltpu.CompilerParams(
            collective_id=0, has_side_effects=True, vmem_limit_bytes=62 * 1024 * 1024
        ),
        cost_estimate=pl.CostEstimate(
            flops=2_500_000_000, bytes_accessed=8_000_000, transcendentals=0
        ),
        name="section",
    )(coarse, up_weight, up_bias, mix_weight, mix_bias)


def solution(mesh):
    placed = (
        P("tile", None, None, "filt"),
        P("filt", None),
        P("filt"),
        P(None, "filt", None),
        P("filt"),
    )
    return jax.shard_map(
        local, mesh=mesh, in_specs=placed, out_specs=P("tile", None, None, "filt"), check_vma=False
    )
```

```python
import jax
import jax.numpy as jnp
from jax import lax
from jax.experimental import pallas as pl
from jax.experimental.pallas import tpu as pltpu
from jax.sharding import PartitionSpec as P

MESH = pl.DeviceIdType.MESH
NT = (((1,), (1,)), ((), ()))

TAPS = (((-1, 3), (0, 1)), ((0, 2), (1, 0)))


def dot_nt(a, b):
    return lax.dot_general(a, b, NT, preferred_element_type=jnp.float32)


def side_by_side(ref, at, cin):
    return jnp.concatenate([ref[:, s : s + cin] for s in at], axis=1)


def kernel(
    coarse, upw, upb, mixw, mixb, out,
    own, cmain, ctail, wup, wd, wmix, ub, mb, xb, hid, scr, acc,
    up_sem, mix_sem, bias_sem, own_sem, send_sem, recv_sem, hand_send, hand_recv, hsend, hrecv,
):
    tiles = lax.axis_size("tile")
    t = lax.axis_index("tile")
    c = lax.axis_index("filt")
    other = 1 - c
    right = t + 1
    left = t - 1
    zl, xl, cs = coarse.shape[1:]
    f = upw.shape[0]
    cin = 2 * cs
    targets = ((t, other), (right, c), (right, other), (left, c), (left, other))
    slots = (1, 0, 0, 2, 2)

    has_left = t > 0
    has_right = t < tiles - 1

    corner = jnp.logical_and(t == 0, c == 0)
    hands_on = jnp.logical_and(t == 0, c == 1)

    def each(action, to_right, to_left):
        @pl.when(to_right)
        def _():
            action(1)
            action(2)

        for k, core in ((3, c), (4, other)):

            @pl.when(to_left(core))
            def _(k=k):
                action(k)

        action(0)

    def sends_left(core):
        return jnp.logical_or(t > 1, jnp.logical_and(t == 1, core == 1))

    barrier = pltpu.get_barrier_semaphore()
    each(
        lambda k: pl.semaphore_signal(
            barrier, inc=1, device_id=targets[k], device_id_type=MESH
        ),
        jnp.logical_and(has_right, jnp.logical_not(corner)),
        lambda core: has_left,
    )

    own_copies = [
        pltpu.make_async_copy(coarse.at[0], own, own_sem.at[0]),
        pltpu.make_async_copy(coarse.at[0, :, :, 0:128], cmain.at[1, c], own_sem.at[1]),
    ]
    for copy in own_copies:
        copy.start()
    bias_copies = [
        pltpu.make_async_copy(upb, ub, bias_sem.at[0]),
        pltpu.make_async_copy(mixb, mb, bias_sem.at[1]),
    ]
    up_copies = {}
    for kx in range(4):
        for ky in range(4):
            cols = pl.ds((16 * ky + 4 * kx) * cin, 4 * cin)
            up_copies[ky, kx] = pltpu.make_async_copy(
                upw.at[:, cols], wup.at[:, cols], up_sem.at[4 * ky + kx]
            )
    up_groups = [[up_copies[ky, kx] for _, kx in TAPS[px] for ky in range(4)] for px in (0, 1)]
    mix_copies = [
        pltpu.make_async_copy(
            mixw.at[:, :, pl.ds(pl.multiple_of(src * f, f), f)], wmix.at[half], mix_sem.at[half]
        )
        for half, src in ((0, c), (1, other))
    ]
    for copy in up_groups[0]:
        copy.start()

    @pl.when(jnp.logical_not(has_left))
    def _():
        cmain[0] = jnp.zeros_like(cmain[0])
        ctail[0] = jnp.zeros_like(ctail[0])

    @pl.when(jnp.logical_not(has_right))
    def _():
        cmain[2] = jnp.zeros_like(cmain[2])
        ctail[2] = jnp.zeros_like(ctail[2])

    first = has_left.astype(jnp.int32)
    last = has_right.astype(jnp.int32)
    @pl.when(c >= 0)
    def _():
        own_copies[1].wait()
        own_copies[0].wait()
        tail = own[:, :, 128:cs].astype(jnp.float32)
        for i in range(zl // 4):
            ctail[1, c, i] = jnp.concatenate(
                [tail[4 * i + j] for j in range(4)], axis=-1
            ).astype(jnp.bfloat16)

    pl.semaphore_wait(barrier, 1 + 2 * first + 2 * last - (t == 1).astype(jnp.int32))
    sends = [
        [
            pltpu.make_async_remote_copy(
                src_ref=src,
                dst_ref=dst,
                send_sem=send_sem.at[part, k],
                recv_sem=recv_sem.at[part, k],
                device_id=dev,
                device_id_type=MESH,
            )
            for part, (src, dst) in enumerate(
                (
                    (cmain.at[1, c], cmain.at[slot, c]),
                    (ctail.at[1, c], ctail.at[slot, c]),
                )
            )
        ]
        for k, (dev, slot) in enumerate(zip(targets, slots))
    ]
    each(lambda k: sends[k][0].start(), has_right, sends_left)
    for copy in (*up_groups[1], *mix_copies, *bias_copies):
        copy.start()

    each(lambda k: sends[k][1].start(), has_right, sends_left)

    handed = [
        pltpu.make_async_remote_copy(
            src_ref=buf.at[2],
            dst_ref=buf.at[2],
            send_sem=hand_send.at[part],
            recv_sem=hand_recv.at[part],
            device_id=(t, other),
            device_id_type=MESH,
        )
        for part, buf in enumerate((cmain, ctail))
    ]

    def arrived(*which):
        for k in which:
            sends[k][0].wait_recv()
            sends[k][1].wait_recv()

    @pl.when(hands_on)
    def _():
        arrived(3, 4)
        for copy in handed:
            copy.start()

    xb[:, :, :, 0] = jnp.zeros_like(xb[:, :, :, 0])
    xb[:, :, :, zl + 1] = jnp.zeros_like(xb[:, :, :, zl + 1])
    hid[:, :, 0] = jnp.zeros_like(hid[:, :, 0])
    hid[:, :, 2 * zl + 1] = jnp.zeros_like(hid[:, :, 2 * zl + 1])
    first = first.astype(jnp.float32)
    last = last.astype(jnp.float32)

    def place(slot):
        parts = []
        for half in (0, 1):
            parts.append(cmain[slot, half])
            packed = ctail[slot, half]
            tails = [
                packed[z // 4, :, (z % 4) * 32 : (z % 4) * 32 + 32] for z in range(zl)
            ]
            parts.append(jnp.stack(tails, axis=0))
        x = jnp.concatenate(parts, axis=-1)
        gap = jnp.zeros((zl, xl, 64), jnp.bfloat16)
        edge = jnp.zeros((zl, 1, cin + 64), jnp.float32)
        for v, parts in enumerate(([gap, x], [x, gap])):
            y = jnp.concatenate(parts, axis=-1).astype(jnp.float32)
            low = jnp.concatenate([edge, y[:, :-1]], axis=1)
            high = jnp.concatenate([y[:, 1:], edge], axis=1)
            for s, w in enumerate((low, y, high)):
                xb[v, s, slot, 1 : zl + 1] = w.astype(jnp.bfloat16)

    arrived(0)
    place(1)

    def pair(px, ky, kz):
        return ((px * 4 + ky) * 4 + kz) * 2 * cin

    def join(px):
        (_, ka), (_, kb) = TAPS[px]
        for ky in range(4):
            for kz in range(4):
                at = [(16 * ky + 4 * kx + kz) * cin for kx in (ka, kb)]
                start = pair(px, ky, kz)
                wd[:, start : start + 2 * cin] = side_by_side(wup, at, cin)

    for px in (0, 1):
        for copy in up_groups[px]:
            copy.wait()

        @pl.when(c >= 0)
        def _(px=px):
            join(px)

    for copy in (*bias_copies, *mix_copies):
        copy.wait()
    ubias = ub[...].astype(jnp.float32).reshape(1, 1, 1, f)
    mbias = mb[...].astype(jnp.float32).reshape(1, f)

    @pl.when(has_left)
    def _():
        arrived(1, 2)

    @pl.when(jnp.logical_and(has_right, t > 0))
    def _():
        arrived(3, 4)

    @pl.when(corner)
    def _():
        for copy in handed:
            copy.wait_recv()

    place(0)
    place(2)

    m = 2 * zl * xl
    swaps = []
    for px in (0, 1):
        for pz in (0, 1):
            lhs, even, odd = [], [], []
            for yt in (0, 1):
                for dz, kz in TAPS[pz]:
                    near, far = [
                        xb[v, dx + 1, yt : yt + 2, dz + 1 : dz + 1 + zl].reshape(m, cin + 64)
                        for v, (dx, _) in zip((1, 0), TAPS[px])
                    ]
                    lhs += [near[:, :256], near[:, 256:] + far[:, :128], far[:, 128:]]
                    for ky, group in ((2 - 2 * yt, even), (3 - 2 * yt, odd)):
                        start = pair(px, ky, kz)
                        group.append(wd[:, start : start + 2 * cin])
            rhs = jnp.concatenate(
                [jnp.concatenate(even, axis=1), jnp.concatenate(odd, axis=1)], axis=0
            )
            up = dot_nt(jnp.concatenate(lhs, axis=1), rhs)
            for q in (0, 1):
                for j in (0, 1):
                    r = 2 * j + q
                    h = up[j * zl * xl : (j + 1) * zl * xl, q * f : (q + 1) * f]
                    h = h.reshape(zl, xl, f) + ubias[0]
                    if r == 0:
                        h = h * first
                    if r == 3:
                        h = h * last
                    edge = jnp.zeros((zl, 1, f), jnp.float32)
                    if px:
                        moved = jnp.concatenate([edge, h[:, :-1]], axis=1)
                    else:
                        moved = jnp.concatenate([h[:, 1:], edge], axis=1)
                    h = h.astype(jnp.bfloat16)
                    moved = moved.astype(jnp.bfloat16)
                    for i in range(zl):
                        zz = 1 + 2 * i + pz
                        hid[0, r, zz, :, (1 + px) * f : (2 + px) * f] = h[i]
                        lane = 0 if px else 3 * f
                        hid[0, r, zz, :, lane : lane + f] = moved[i]
        copy = pltpu.make_async_remote_copy(
            src_ref=hid.at[0, :, pl.ds(1, 2 * zl), :, pl.ds((1 + px) * f, f)],
            dst_ref=hid.at[1, :, pl.ds(1, 2 * zl), :, pl.ds((1 + px) * f, f)],
            send_sem=hsend.at[px],
            recv_sem=hrecv.at[px],
            device_id=(t, other),
            device_id_type=MESH,
        )
        copy.start()
        swaps.append(copy)

    def window(half, r, dz, xs):
        lanes = slice(xs[0] * f, (xs[-1] + 1) * f)
        return hid[half, r, dz : dz + 2 * zl, :, lanes].reshape(m, len(xs) * f)

    def tap(half, a, p, r, x, dz):
        dy, dx = r - a, x - p
        if 0 <= dy < 3 and 0 <= dx < 3:
            return wmix[half, 9 * dy + 3 * dx + dz]
        return jnp.zeros((f, f), jnp.bfloat16)

    groups = (
        ((1, 2), (1, 2), ((0, 0), (0, 1), (1, 0), (1, 1))),
        ((0,), (1, 2), ((0, 0), (0, 1))),
        ((3,), (1, 2), ((1, 0), (1, 1))),
        ((0, 1, 2, 3), (0,), ((0, 0), (1, 0))),
        ((0, 1, 2, 3), (3,), ((0, 1), (1, 1))),
    )

    def mix(half):
        parts = {}
        for rows, xs, outs in groups:
            steps = [(r, dz) for r in rows for dz in range(3)]
            lhs = jnp.concatenate([window(half, r, dz, xs) for r, dz in steps], axis=1)
            rhs = jnp.concatenate(
                [
                    jnp.concatenate(
                        [tap(half, a, p, r, x, dz) for r, dz in steps for x in xs], axis=1
                    )
                    for a, p in outs
                ],
                axis=0,
            )
            got = dot_nt(lhs, rhs)
            for i, key in enumerate(outs):
                part = got[:, i * f : (i + 1) * f]
                parts[key] = parts[key] + part if key in parts else part
        return parts

    @pl.when(c >= 0)
    def _():
        for (a, p), part in mix(0).items():
            acc[a, p] = part

    for copy in swaps:
        copy.wait_recv()
    for px in (0, 1):
        for r in range(4):
            h = hid[1, r, 1 : 2 * zl + 1, :, (1 + px) * f : (2 + px) * f].astype(jnp.float32)
            edge = jnp.zeros((2 * zl, 1, f), jnp.float32)
            if px:
                moved = jnp.concatenate([edge, h[:, :-1]], axis=1)
            else:
                moved = jnp.concatenate([h[:, 1:], edge], axis=1)
            lane = 0 if px else 3 * f
            hid[1, r, 1 : 2 * zl + 1, :, lane : lane + f] = moved.astype(jnp.bfloat16)
    rest = mix(1)

    for a in (0, 1):
        for p in (0, 1):
            y = acc[a, p] + rest[a, p] + mbias
            y = jnp.maximum(y, 0.0).reshape(2 * zl, xl, f)
            scr[:, pl.ds(p, xl, stride=2), :] = y
        out[a] = scr[...].astype(jnp.bfloat16)

    each(
        lambda k: (sends[k][0].wait_send(), sends[k][1].wait_send()), has_right, sends_left
    )

    @pl.when(hands_on)
    def _():
        for copy in handed:
            copy.wait_send()

    for copy in swaps:
        copy.wait_send()


def local(coarse, up_weight, up_bias, mix_weight, mix_bias):
    _, zl, xl, cs = coarse.shape
    f = up_weight.shape[0]
    bf16 = jnp.bfloat16
    anywhere = pl.BlockSpec(memory_space=pl.ANY)
    return pl.pallas_call(
        kernel,
        out_shape=pltpu.VMEM((2, 2 * zl, 2 * xl, f), bf16),
        in_specs=[pl.BlockSpec(memory_space=pltpu.HBM)] * 5,
        out_specs=pl.BlockSpec(memory_space=pltpu.VMEM),
        scratch_shapes=[
            pltpu.VMEM((zl, xl, cs), bf16),
            pltpu.VMEM((3, 2, zl, xl, 128), bf16),
            pltpu.VMEM((3, 2, zl // 4, xl, 128), bf16),
            pltpu.VMEM(up_weight.shape, bf16),
            pltpu.VMEM(up_weight.shape, bf16),
            pltpu.VMEM((2, 27, f, f), bf16),
            pltpu.VMEM((f,), bf16),
            pltpu.VMEM((f,), bf16),
            pltpu.VMEM((2, 3, 3, zl + 2, xl, 2 * cs + 64), bf16),
            pltpu.VMEM((2, 4, 2 * zl + 2, xl, 4 * f), bf16),
            pltpu.VMEM((2 * zl, 2 * xl, f), jnp.float32),
            pltpu.VMEM((2, 2, 2 * zl * xl, f), jnp.float32),
            pltpu.SemaphoreType.DMA((16,)),
            pltpu.SemaphoreType.DMA((2,)),
            pltpu.SemaphoreType.DMA((2,)),
            pltpu.SemaphoreType.DMA((2,)),
            pltpu.SemaphoreType.DMA((2, 5)),
            pltpu.SemaphoreType.DMA((2, 5)),
            pltpu.SemaphoreType.DMA((2,)),
            pltpu.SemaphoreType.DMA((2,)),
            pltpu.SemaphoreType.DMA((2,)),
            pltpu.SemaphoreType.DMA((2,)),
        ],
        compiler_params=pltpu.CompilerParams(
            collective_id=0, has_side_effects=True, vmem_limit_bytes=62 * 1024 * 1024
        ),
        cost_estimate=pl.CostEstimate(
            flops=2_500_000_000, bytes_accessed=8_000_000, transcendentals=0
        ),
        name="section",
    )(coarse, up_weight, up_bias, mix_weight, mix_bias)


def solution(mesh):
    placed = (
        P("tile", None, None, "filt"),
        P("filt", None),
        P("filt"),
        P(None, "filt", None),
        P("filt"),
    )
    return jax.shard_map(
        local, mesh=mesh, in_specs=placed, out_specs=P("tile", None, None, "filt"), check_vma=False
    )
```

```python
import jax
import jax.numpy as jnp
from jax import lax
from jax.experimental import pallas as pl
from jax.experimental.pallas import tpu as pltpu
from jax.sharding import PartitionSpec as P

MESH = pl.DeviceIdType.MESH
NT = (((1,), (1,)), ((), ()))

TAPS = (((-1, 3), (0, 1)), ((0, 2), (1, 0)))


def dot_nt(a, b):
    return lax.dot_general(a, b, NT, preferred_element_type=jnp.float32)


def side_by_side(ref, at, cin):
    return jnp.concatenate([ref[:, s : s + cin] for s in at], axis=1)


def kernel(
    coarse, upw, upb, mixw, mixb, out,
    own, cmain, ctail, wup, wd, wmix, ub, mb, xb, hid, scr, acc,
    up_sem, mix_sem, bias_sem, own_sem, send_sem, recv_sem, hand_send, hand_recv, hsend, hrecv,
):
    tiles = lax.axis_size("tile")
    t = lax.axis_index("tile")
    c = lax.axis_index("filt")
    other = 1 - c
    right = t + 1
    left = t - 1
    zl, xl, cs = coarse.shape[1:]
    f = upw.shape[0]
    cin = 2 * cs
    targets = ((t, other), (right, c), (right, other), (left, c), (left, other))
    slots = (1, 0, 0, 2, 2)

    has_left = t > 0
    has_right = t < tiles - 1

    corner = jnp.logical_and(t == 0, c == 0)
    hands_on = jnp.logical_and(t == 0, c == 1)

    def each(action, to_right, to_left):
        @pl.when(to_right)
        def _():
            action(1)
            action(2)

        for k, core in ((3, c), (4, other)):

            @pl.when(to_left(core))
            def _(k=k):
                action(k)

        action(0)

    def sends_left(core):
        return jnp.logical_or(t > 1, jnp.logical_and(t == 1, core == 1))

    barrier = pltpu.get_barrier_semaphore()
    each(
        lambda k: pl.semaphore_signal(
            barrier, inc=1, device_id=targets[k], device_id_type=MESH
        ),
        jnp.logical_and(has_right, jnp.logical_not(corner)),
        lambda core: has_left,
    )

    own_copies = [
        pltpu.make_async_copy(coarse.at[0], own, own_sem.at[0]),
        pltpu.make_async_copy(coarse.at[0, :, :, 0:128], cmain.at[1, c], own_sem.at[1]),
    ]
    for copy in own_copies:
        copy.start()
    bias_copies = [
        pltpu.make_async_copy(upb, ub, bias_sem.at[0]),
        pltpu.make_async_copy(mixb, mb, bias_sem.at[1]),
    ]
    up_copies = {}
    for kx in range(4):
        for ky in range(4):
            cols = pl.ds((16 * ky + 4 * kx) * cin, 4 * cin)
            up_copies[ky, kx] = pltpu.make_async_copy(
                upw.at[:, cols], wup.at[:, cols], up_sem.at[4 * ky + kx]
            )
    up_groups = [[up_copies[ky, kx] for _, kx in TAPS[px] for ky in range(4)] for px in (0, 1)]
    mix_copies = [
        pltpu.make_async_copy(
            mixw.at[:, :, pl.ds(pl.multiple_of(src * f, f), f)], wmix.at[half], mix_sem.at[half]
        )
        for half, src in ((0, c), (1, other))
    ]

    @pl.when(corner)
    def _():
        for copy in (*up_groups[0], *up_groups[1], *mix_copies, *bias_copies):
            copy.start()

    @pl.when(jnp.logical_not(has_left))
    def _():
        cmain[0] = jnp.zeros_like(cmain[0])
        ctail[0] = jnp.zeros_like(ctail[0])

    @pl.when(jnp.logical_not(has_right))
    def _():
        cmain[2] = jnp.zeros_like(cmain[2])
        ctail[2] = jnp.zeros_like(ctail[2])

    first = has_left.astype(jnp.int32)
    last = has_right.astype(jnp.int32)
    @pl.when(c >= 0)
    def _():
        own_copies[1].wait()
        own_copies[0].wait()
        tail = own[:, :, 128:cs].astype(jnp.float32)
        for i in range(zl // 4):
            ctail[1, c, i] = jnp.concatenate(
                [tail[4 * i + j] for j in range(4)], axis=-1
            ).astype(jnp.bfloat16)

    @pl.when(jnp.logical_not(corner))
    def _():
        for copy in up_groups[0]:
            copy.start()

    pl.semaphore_wait(barrier, 1 + 2 * first + 2 * last - (t == 1).astype(jnp.int32))
    sends = [
        [
            pltpu.make_async_remote_copy(
                src_ref=src,
                dst_ref=dst,
                send_sem=send_sem.at[part, k],
                recv_sem=recv_sem.at[part, k],
                device_id=dev,
                device_id_type=MESH,
            )
            for part, (src, dst) in enumerate(
                (
                    (cmain.at[1, c], cmain.at[slot, c]),
                    (ctail.at[1, c], ctail.at[slot, c]),
                )
            )
        ]
        for k, (dev, slot) in enumerate(zip(targets, slots))
    ]
    each(lambda k: sends[k][0].start(), has_right, sends_left)

    @pl.when(jnp.logical_not(corner))
    def _():
        for copy in (*up_groups[1], *mix_copies, *bias_copies):
            copy.start()


    each(lambda k: sends[k][1].start(), has_right, sends_left)

    handed = [
        pltpu.make_async_remote_copy(
            src_ref=buf.at[2],
            dst_ref=buf.at[2],
            send_sem=hand_send.at[part],
            recv_sem=hand_recv.at[part],
            device_id=(t, other),
            device_id_type=MESH,
        )
        for part, buf in enumerate((cmain, ctail))
    ]

    def arrived(*which):
        for k in which:
            sends[k][0].wait_recv()
            sends[k][1].wait_recv()

    @pl.when(hands_on)
    def _():
        arrived(3, 4)
        for copy in handed:
            copy.start()

    xb[:, :, :, 0] = jnp.zeros_like(xb[:, :, :, 0])
    xb[:, :, :, zl + 1] = jnp.zeros_like(xb[:, :, :, zl + 1])
    hid[:, :, 0] = jnp.zeros_like(hid[:, :, 0])
    hid[:, :, 2 * zl + 1] = jnp.zeros_like(hid[:, :, 2 * zl + 1])
    first = first.astype(jnp.float32)
    last = last.astype(jnp.float32)

    def place(slot):
        parts = []
        for half in (0, 1):
            parts.append(cmain[slot, half])
            packed = ctail[slot, half]
            tails = [
                packed[z // 4, :, (z % 4) * 32 : (z % 4) * 32 + 32] for z in range(zl)
            ]
            parts.append(jnp.stack(tails, axis=0))
        x = jnp.concatenate(parts, axis=-1)
        gap = jnp.zeros((zl, xl, 64), jnp.bfloat16)
        edge = jnp.zeros((zl, 1, cin + 64), jnp.float32)
        for v, parts in enumerate(([gap, x], [x, gap])):
            y = jnp.concatenate(parts, axis=-1).astype(jnp.float32)
            low = jnp.concatenate([edge, y[:, :-1]], axis=1)
            high = jnp.concatenate([y[:, 1:], edge], axis=1)
            for s, w in enumerate((low, y, high)):
                xb[v, s, slot, 1 : zl + 1] = w.astype(jnp.bfloat16)

    arrived(0)
    place(1)

    def pair(px, ky, kz):
        return ((px * 4 + ky) * 4 + kz) * 2 * cin

    def join(px):
        (_, ka), (_, kb) = TAPS[px]
        for ky in range(4):
            for kz in range(4):
                at = [(16 * ky + 4 * kx + kz) * cin for kx in (ka, kb)]
                start = pair(px, ky, kz)
                wd[:, start : start + 2 * cin] = side_by_side(wup, at, cin)

    for px in (0, 1):
        for copy in up_groups[px]:
            copy.wait()

        @pl.when(c >= 0)
        def _(px=px):
            join(px)

    for copy in (*bias_copies, *mix_copies):
        copy.wait()
    ubias = ub[...].astype(jnp.float32).reshape(1, 1, 1, f)
    mbias = mb[...].astype(jnp.float32).reshape(1, f)

    @pl.when(has_left)
    def _():
        arrived(1, 2)

    @pl.when(jnp.logical_and(has_right, t > 0))
    def _():
        arrived(3, 4)

    @pl.when(corner)
    def _():
        for copy in handed:
            copy.wait_recv()

    place(0)
    place(2)

    m = 2 * zl * xl
    swaps = []
    for px in (0, 1):
        for pz in (0, 1):
            lhs, even, odd = [], [], []
            for yt in (0, 1):
                for dz, kz in TAPS[pz]:
                    near, far = [
                        xb[v, dx + 1, yt : yt + 2, dz + 1 : dz + 1 + zl].reshape(m, cin + 64)
                        for v, (dx, _) in zip((1, 0), TAPS[px])
                    ]
                    lhs += [near[:, :256], near[:, 256:] + far[:, :128], far[:, 128:]]
                    for ky, group in ((2 - 2 * yt, even), (3 - 2 * yt, odd)):
                        start = pair(px, ky, kz)
                        group.append(wd[:, start : start + 2 * cin])
            rhs = jnp.concatenate(
                [jnp.concatenate(even, axis=1), jnp.concatenate(odd, axis=1)], axis=0
            )
            up = dot_nt(jnp.concatenate(lhs, axis=1), rhs)
            for q in (0, 1):
                for j in (0, 1):
                    r = 2 * j + q
                    h = up[j * zl * xl : (j + 1) * zl * xl, q * f : (q + 1) * f]
                    h = h.reshape(zl, xl, f) + ubias[0]
                    if r == 0:
                        h = h * first
                    if r == 3:
                        h = h * last
                    edge = jnp.zeros((zl, 1, f), jnp.float32)
                    if px:
                        moved = jnp.concatenate([edge, h[:, :-1]], axis=1)
                    else:
                        moved = jnp.concatenate([h[:, 1:], edge], axis=1)
                    h = h.astype(jnp.bfloat16)
                    moved = moved.astype(jnp.bfloat16)
                    for i in range(zl):
                        zz = 1 + 2 * i + pz
                        hid[0, r, zz, :, (1 + px) * f : (2 + px) * f] = h[i]
                        lane = 0 if px else 3 * f
                        hid[0, r, zz, :, lane : lane + f] = moved[i]
        copy = pltpu.make_async_remote_copy(
            src_ref=hid.at[0, :, pl.ds(1, 2 * zl), :, pl.ds((1 + px) * f, f)],
            dst_ref=hid.at[1, :, pl.ds(1, 2 * zl), :, pl.ds((1 + px) * f, f)],
            send_sem=hsend.at[px],
            recv_sem=hrecv.at[px],
            device_id=(t, other),
            device_id_type=MESH,
        )
        copy.start()
        swaps.append(copy)

    def window(half, r, dz, xs):
        lanes = slice(xs[0] * f, (xs[-1] + 1) * f)
        return hid[half, r, dz : dz + 2 * zl, :, lanes].reshape(m, len(xs) * f)

    def tap(half, a, p, r, x, dz):
        dy, dx = r - a, x - p
        if 0 <= dy < 3 and 0 <= dx < 3:
            return wmix[half, 9 * dy + 3 * dx + dz]
        return jnp.zeros((f, f), jnp.bfloat16)

    groups = (
        ((1, 2), (1, 2), ((0, 0), (0, 1), (1, 0), (1, 1))),
        ((0,), (1, 2), ((0, 0), (0, 1))),
        ((3,), (1, 2), ((1, 0), (1, 1))),
        ((0, 1, 2, 3), (0,), ((0, 0), (1, 0))),
        ((0, 1, 2, 3), (3,), ((0, 1), (1, 1))),
    )

    def mix(half, groups):
        parts = {}
        for rows, xs, outs in groups:
            steps = [(r, dz) for r in rows for dz in range(3)]
            lhs = jnp.concatenate([window(half, r, dz, xs) for r, dz in steps], axis=1)
            rhs = jnp.concatenate(
                [
                    jnp.concatenate(
                        [tap(half, a, p, r, x, dz) for r, dz in steps for x in xs], axis=1
                    )
                    for a, p in outs
                ],
                axis=0,
            )
            got = dot_nt(lhs, rhs)
            for i, key in enumerate(outs):
                part = got[:, i * f : (i + 1) * f]
                parts[key] = parts[key] + part if key in parts else part
        return parts

    @pl.when(c >= 0)
    def _():
        for (a, p), part in mix(0, groups).items():
            acc[a, p] = part

    def widen(px):
        for r in range(4):
            h = hid[1, r, 1 : 2 * zl + 1, :, (1 + px) * f : (2 + px) * f].astype(jnp.float32)
            edge = jnp.zeros((2 * zl, 1, f), jnp.float32)
            if px:
                moved = jnp.concatenate([edge, h[:, :-1]], axis=1)
            else:
                moved = jnp.concatenate([h[:, 1:], edge], axis=1)
            lane = 0 if px else 3 * f
            hid[1, r, 1 : 2 * zl + 1, :, lane : lane + f] = moved.astype(jnp.bfloat16)

    swaps[0].wait_recv()

    @pl.when(c >= 0)
    def _():
        widen(0)
        for (a, p), part in mix(1, groups[-1:]).items():
            acc[a, p] += part

    swaps[1].wait_recv()
    widen(1)
    rest = mix(1, groups[:-1])

    for a in (0, 1):
        for p in (0, 1):
            y = acc[a, p] + rest[a, p] + mbias
            y = jnp.maximum(y, 0.0).reshape(2 * zl, xl, f)
            scr[:, pl.ds(p, xl, stride=2), :] = y
        out[a] = scr[...].astype(jnp.bfloat16)

    each(
        lambda k: (sends[k][0].wait_send(), sends[k][1].wait_send()), has_right, sends_left
    )

    @pl.when(hands_on)
    def _():
        for copy in handed:
            copy.wait_send()

    for copy in swaps:
        copy.wait_send()


def local(coarse, up_weight, up_bias, mix_weight, mix_bias):
    _, zl, xl, cs = coarse.shape
    f = up_weight.shape[0]
    bf16 = jnp.bfloat16
    anywhere = pl.BlockSpec(memory_space=pl.ANY)
    return pl.pallas_call(
        kernel,
        out_shape=pltpu.VMEM((2, 2 * zl, 2 * xl, f), bf16),
        in_specs=[pl.BlockSpec(memory_space=pltpu.HBM)] * 5,
        out_specs=pl.BlockSpec(memory_space=pltpu.VMEM),
        scratch_shapes=[
            pltpu.VMEM((zl, xl, cs), bf16),
            pltpu.VMEM((3, 2, zl, xl, 128), bf16),
            pltpu.VMEM((3, 2, zl // 4, xl, 128), bf16),
            pltpu.VMEM(up_weight.shape, bf16),
            pltpu.VMEM(up_weight.shape, bf16),
            pltpu.VMEM((2, 27, f, f), bf16),
            pltpu.VMEM((f,), bf16),
            pltpu.VMEM((f,), bf16),
            pltpu.VMEM((2, 3, 3, zl + 2, xl, 2 * cs + 64), bf16),
            pltpu.VMEM((2, 4, 2 * zl + 2, xl, 4 * f), bf16),
            pltpu.VMEM((2 * zl, 2 * xl, f), jnp.float32),
            pltpu.VMEM((2, 2, 2 * zl * xl, f), jnp.float32),
            pltpu.SemaphoreType.DMA((16,)),
            pltpu.SemaphoreType.DMA((2,)),
            pltpu.SemaphoreType.DMA((2,)),
            pltpu.SemaphoreType.DMA((2,)),
            pltpu.SemaphoreType.DMA((2, 5)),
            pltpu.SemaphoreType.DMA((2, 5)),
            pltpu.SemaphoreType.DMA((2,)),
            pltpu.SemaphoreType.DMA((2,)),
            pltpu.SemaphoreType.DMA((2,)),
            pltpu.SemaphoreType.DMA((2,)),
        ],
        compiler_params=pltpu.CompilerParams(
            collective_id=0, has_side_effects=True, vmem_limit_bytes=62 * 1024 * 1024
        ),
        cost_estimate=pl.CostEstimate(
            flops=2_500_000_000, bytes_accessed=8_000_000, transcendentals=0
        ),
        name="section",
    )(coarse, up_weight, up_bias, mix_weight, mix_bias)


def solution(mesh):
    placed = (
        P("tile", None, None, "filt"),
        P("filt", None),
        P("filt"),
        P(None, "filt", None),
        P("filt"),
    )
    return jax.shard_map(
        local, mesh=mesh, in_specs=placed, out_specs=P("tile", None, None, "filt"), check_vma=False
    )
```

```python
import jax
import jax.numpy as jnp
from jax import lax
from jax.experimental import pallas as pl
from jax.experimental.pallas import tpu as pltpu
from jax.sharding import PartitionSpec as P

MESH = pl.DeviceIdType.MESH
NT = (((1,), (1,)), ((), ()))

TAPS = (((-1, 3), (0, 1)), ((0, 2), (1, 0)))


def dot_nt(a, b):
    return lax.dot_general(a, b, NT, preferred_element_type=jnp.float32)


def side_by_side(ref, at, cin):
    return jnp.concatenate([ref[:, s : s + cin] for s in at], axis=1)


def kernel(
    coarse, upw, upb, mixw, mixb, out,
    own, cmain, ctail, wup, wd, wmix, ub, mb, xb, hid, scr, acc,
    up_sem, mix_sem, bias_sem, own_sem, send_sem, recv_sem, hand_send, hand_recv, hsend, hrecv,
):
    tiles = lax.axis_size("tile")
    t = lax.axis_index("tile")
    c = lax.axis_index("filt")
    other = 1 - c
    right = t + 1
    left = t - 1
    zl, xl, cs = coarse.shape[1:]
    f = upw.shape[0]
    cin = 2 * cs
    targets = ((t, other), (right, c), (right, other), (left, c), (left, other))
    slots = (1, 0, 0, 2, 2)

    has_left = t > 0
    has_right = t < tiles - 1

    corner = jnp.logical_and(t == 0, c == 0)
    hands_on = jnp.logical_and(t == 0, c == 1)

    def each(action, to_right, to_left):
        @pl.when(to_right)
        def _():
            action(1)
            action(2)

        for k, core in ((3, c), (4, other)):

            @pl.when(to_left(core))
            def _(k=k):
                action(k)

        action(0)

    def sends_left(core):
        return jnp.logical_or(t > 1, jnp.logical_and(t == 1, core == 1))

    barrier = pltpu.get_barrier_semaphore()
    each(
        lambda k: pl.semaphore_signal(
            barrier, inc=1, device_id=targets[k], device_id_type=MESH
        ),
        jnp.logical_and(has_right, jnp.logical_not(corner)),
        lambda core: has_left,
    )

    own_copies = [
        pltpu.make_async_copy(coarse.at[0], own, own_sem.at[0]),
        pltpu.make_async_copy(coarse.at[0, :, :, 0:128], cmain.at[1, c], own_sem.at[1]),
    ]
    for copy in own_copies:
        copy.start()
    bias_copies = [
        pltpu.make_async_copy(upb, ub, bias_sem.at[0]),
        pltpu.make_async_copy(mixb, mb, bias_sem.at[1]),
    ]
    up_copies = {}
    for kx in range(4):
        for ky in range(4):
            cols = pl.ds((16 * ky + 4 * kx) * cin, 4 * cin)
            up_copies[ky, kx] = pltpu.make_async_copy(
                upw.at[:, cols], wup.at[:, cols], up_sem.at[4 * ky + kx]
            )
    up_groups = [[up_copies[ky, kx] for _, kx in TAPS[px] for ky in range(4)] for px in (0, 1)]
    mix_copies = [
        pltpu.make_async_copy(
            mixw.at[:, :, pl.ds(pl.multiple_of(src * f, f), f)], wmix.at[half], mix_sem.at[half]
        )
        for half, src in ((0, c), (1, other))
    ]

    @pl.when(jnp.logical_not(has_left))
    def _():
        cmain[0] = jnp.zeros_like(cmain[0])
        ctail[0] = jnp.zeros_like(ctail[0])

    @pl.when(jnp.logical_not(has_right))
    def _():
        cmain[2] = jnp.zeros_like(cmain[2])
        ctail[2] = jnp.zeros_like(ctail[2])

    first = has_left.astype(jnp.int32)
    last = has_right.astype(jnp.int32)
    @pl.when(c >= 0)
    def _():
        own_copies[1].wait()
        own_copies[0].wait()
        tail = own[:, :, 128:cs].astype(jnp.float32)
        for i in range(zl // 4):
            ctail[1, c, i] = jnp.concatenate(
                [tail[4 * i + j] for j in range(4)], axis=-1
            ).astype(jnp.bfloat16)

    for copy in up_groups[0]:
        copy.start()
    pl.semaphore_wait(barrier, 1 + 2 * first + 2 * last - (t == 1).astype(jnp.int32))
    sends = [
        [
            pltpu.make_async_remote_copy(
                src_ref=src,
                dst_ref=dst,
                send_sem=send_sem.at[part, k],
                recv_sem=recv_sem.at[part, k],
                device_id=dev,
                device_id_type=MESH,
            )
            for part, (src, dst) in enumerate(
                (
                    (cmain.at[1, c], cmain.at[slot, c]),
                    (ctail.at[1, c], ctail.at[slot, c]),
                )
            )
        ]
        for k, (dev, slot) in enumerate(zip(targets, slots))
    ]
    each(lambda k: sends[k][0].start(), has_right, sends_left)
    for copy in (*bias_copies, *up_groups[1], *mix_copies):
        copy.start()

    each(lambda k: sends[k][1].start(), has_right, sends_left)

    handed = [
        pltpu.make_async_remote_copy(
            src_ref=buf.at[2],
            dst_ref=buf.at[2],
            send_sem=hand_send.at[part],
            recv_sem=hand_recv.at[part],
            device_id=(t, other),
            device_id_type=MESH,
        )
        for part, buf in enumerate((cmain, ctail))
    ]

    def arrived(*which):
        for k in which:
            sends[k][0].wait_recv()
            sends[k][1].wait_recv()

    @pl.when(hands_on)
    def _():
        arrived(3, 4)
        for copy in handed:
            copy.start()

    xb[:, :, :, 0] = jnp.zeros_like(xb[:, :, :, 0])
    xb[:, :, :, zl + 1] = jnp.zeros_like(xb[:, :, :, zl + 1])
    hid[:, :, 0] = jnp.zeros_like(hid[:, :, 0])
    hid[:, :, 2 * zl + 1] = jnp.zeros_like(hid[:, :, 2 * zl + 1])
    first = first.astype(jnp.float32)
    last = last.astype(jnp.float32)

    def place(slot):
        parts = []
        for half in (0, 1):
            parts.append(cmain[slot, half])
            packed = ctail[slot, half]
            tails = [
                packed[z // 4, :, (z % 4) * 32 : (z % 4) * 32 + 32] for z in range(zl)
            ]
            parts.append(jnp.stack(tails, axis=0))
        x = jnp.concatenate(parts, axis=-1)
        gap = jnp.zeros((zl, xl, 64), jnp.bfloat16)
        edge = jnp.zeros((zl, 1, cin + 64), jnp.float32)
        for v, parts in enumerate(([gap, x], [x, gap])):
            y = jnp.concatenate(parts, axis=-1).astype(jnp.float32)
            low = jnp.concatenate([edge, y[:, :-1]], axis=1)
            high = jnp.concatenate([y[:, 1:], edge], axis=1)
            for s, w in enumerate((low, y, high)):
                xb[v, s, slot, 1 : zl + 1] = w.astype(jnp.bfloat16)

    arrived(0)
    place(1)

    def pair(px, ky, kz):
        return ((px * 4 + ky) * 4 + kz) * 2 * cin

    def join(px):
        (_, ka), (_, kb) = TAPS[px]
        for ky in range(4):
            for kz in range(4):
                at = [(16 * ky + 4 * kx + kz) * cin for kx in (ka, kb)]
                start = pair(px, ky, kz)
                wd[:, start : start + 2 * cin] = side_by_side(wup, at, cin)

    def ready(px):
        for copy in up_groups[px]:
            copy.wait()
        join(px)

    @pl.when(c >= 0)
    def _():
        ready(0)

    @pl.when(jnp.logical_not(corner))
    def _():
        ready(1)

    for copy in bias_copies:
        copy.wait()
    ubias = ub[...].astype(jnp.float32).reshape(1, 1, 1, f)
    mbias = mb[...].astype(jnp.float32).reshape(1, f)

    @pl.when(has_left)
    def _():
        arrived(1, 2)

    @pl.when(jnp.logical_and(has_right, t > 0))
    def _():
        arrived(3, 4)

    @pl.when(corner)
    def _():
        for copy in handed:
            copy.wait_recv()

    place(0)
    place(2)

    m = 2 * zl * xl
    swaps = []
    for px in (0, 1):
        if px:

            @pl.when(corner)
            def _():
                ready(1)

        for pz in (0, 1):
            lhs, even, odd = [], [], []
            for yt in (0, 1):
                for dz, kz in TAPS[pz]:
                    near, far = [
                        xb[v, dx + 1, yt : yt + 2, dz + 1 : dz + 1 + zl].reshape(m, cin + 64)
                        for v, (dx, _) in zip((1, 0), TAPS[px])
                    ]
                    lhs += [near[:, :256], near[:, 256:] + far[:, :128], far[:, 128:]]
                    for ky, group in ((2 - 2 * yt, even), (3 - 2 * yt, odd)):
                        start = pair(px, ky, kz)
                        group.append(wd[:, start : start + 2 * cin])
            rhs = jnp.concatenate(
                [jnp.concatenate(even, axis=1), jnp.concatenate(odd, axis=1)], axis=0
            )
            up = dot_nt(jnp.concatenate(lhs, axis=1), rhs)
            for q in (0, 1):
                for j in (0, 1):
                    r = 2 * j + q
                    h = up[j * zl * xl : (j + 1) * zl * xl, q * f : (q + 1) * f]
                    h = h.reshape(zl, xl, f) + ubias[0]
                    if r == 0:
                        h = h * first
                    if r == 3:
                        h = h * last
                    edge = jnp.zeros((zl, 1, f), jnp.float32)
                    if px:
                        moved = jnp.concatenate([edge, h[:, :-1]], axis=1)
                    else:
                        moved = jnp.concatenate([h[:, 1:], edge], axis=1)
                    h = h.astype(jnp.bfloat16)
                    moved = moved.astype(jnp.bfloat16)
                    for i in range(zl):
                        zz = 1 + 2 * i + pz
                        hid[0, r, zz, :, (1 + px) * f : (2 + px) * f] = h[i]
                        lane = 0 if px else 3 * f
                        hid[0, r, zz, :, lane : lane + f] = moved[i]
        copy = pltpu.make_async_remote_copy(
            src_ref=hid.at[0, :, pl.ds(1, 2 * zl), :, pl.ds((1 + px) * f, f)],
            dst_ref=hid.at[1, :, pl.ds(1, 2 * zl), :, pl.ds((1 + px) * f, f)],
            send_sem=hsend.at[px],
            recv_sem=hrecv.at[px],
            device_id=(t, other),
            device_id_type=MESH,
        )
        copy.start()
        swaps.append(copy)

    def window(half, r, dz, xs):
        lanes = slice(xs[0] * f, (xs[-1] + 1) * f)
        return hid[half, r, dz : dz + 2 * zl, :, lanes].reshape(m, len(xs) * f)

    def tap(half, a, p, r, x, dz):
        dy, dx = r - a, x - p
        if 0 <= dy < 3 and 0 <= dx < 3:
            return wmix[half, 9 * dy + 3 * dx + dz]
        return jnp.zeros((f, f), jnp.bfloat16)

    groups = (
        ((1, 2), (1, 2), ((0, 0), (0, 1), (1, 0), (1, 1))),
        ((0,), (1, 2), ((0, 0), (0, 1))),
        ((3,), (1, 2), ((1, 0), (1, 1))),
        ((0, 1, 2, 3), (0,), ((0, 0), (1, 0))),
        ((0, 1, 2, 3), (3,), ((0, 1), (1, 1))),
    )

    def mix(half, groups):
        parts = {}
        for rows, xs, outs in groups:
            steps = [(r, dz) for r in rows for dz in range(3)]
            lhs = jnp.concatenate([window(half, r, dz, xs) for r, dz in steps], axis=1)
            rhs = jnp.concatenate(
                [
                    jnp.concatenate(
                        [tap(half, a, p, r, x, dz) for r, dz in steps for x in xs], axis=1
                    )
                    for a, p in outs
                ],
                axis=0,
            )
            got = dot_nt(lhs, rhs)
            for i, key in enumerate(outs):
                part = got[:, i * f : (i + 1) * f]
                parts[key] = parts[key] + part if key in parts else part
        return parts

    for copy in mix_copies:
        copy.wait()

    @pl.when(c >= 0)
    def _():
        for (a, p), part in mix(0, groups).items():
            acc[a, p] = part

    def widen(px):
        for r in range(4):
            h = hid[1, r, 1 : 2 * zl + 1, :, (1 + px) * f : (2 + px) * f].astype(jnp.float32)
            edge = jnp.zeros((2 * zl, 1, f), jnp.float32)
            if px:
                moved = jnp.concatenate([edge, h[:, :-1]], axis=1)
            else:
                moved = jnp.concatenate([h[:, 1:], edge], axis=1)
            lane = 0 if px else 3 * f
            hid[1, r, 1 : 2 * zl + 1, :, lane : lane + f] = moved.astype(jnp.bfloat16)

    swaps[0].wait_recv()

    @pl.when(c >= 0)
    def _():
        widen(0)
        for (a, p), part in mix(1, groups[-1:]).items():
            acc[a, p] += part

    swaps[1].wait_recv()
    widen(1)
    rest = mix(1, groups[:-1])

    for a in (0, 1):
        for p in (0, 1):
            y = acc[a, p] + rest[a, p] + mbias
            y = jnp.maximum(y, 0.0).reshape(2 * zl, xl, f)
            scr[:, pl.ds(p, xl, stride=2), :] = y
        out[a] = scr[...].astype(jnp.bfloat16)

    each(
        lambda k: (sends[k][0].wait_send(), sends[k][1].wait_send()), has_right, sends_left
    )

    @pl.when(hands_on)
    def _():
        for copy in handed:
            copy.wait_send()

    for copy in swaps:
        copy.wait_send()


def local(coarse, up_weight, up_bias, mix_weight, mix_bias):
    _, zl, xl, cs = coarse.shape
    f = up_weight.shape[0]
    bf16 = jnp.bfloat16
    anywhere = pl.BlockSpec(memory_space=pl.ANY)
    return pl.pallas_call(
        kernel,
        out_shape=pltpu.VMEM((2, 2 * zl, 2 * xl, f), bf16),
        in_specs=[pl.BlockSpec(memory_space=pltpu.HBM)] * 5,
        out_specs=pl.BlockSpec(memory_space=pltpu.VMEM),
        scratch_shapes=[
            pltpu.VMEM((zl, xl, cs), bf16),
            pltpu.VMEM((3, 2, zl, xl, 128), bf16),
            pltpu.VMEM((3, 2, zl // 4, xl, 128), bf16),
            pltpu.VMEM(up_weight.shape, bf16),
            pltpu.VMEM(up_weight.shape, bf16),
            pltpu.VMEM((2, 27, f, f), bf16),
            pltpu.VMEM((f,), bf16),
            pltpu.VMEM((f,), bf16),
            pltpu.VMEM((2, 3, 3, zl + 2, xl, 2 * cs + 64), bf16),
            pltpu.VMEM((2, 4, 2 * zl + 2, xl, 4 * f), bf16),
            pltpu.VMEM((2 * zl, 2 * xl, f), jnp.float32),
            pltpu.VMEM((2, 2, 2 * zl * xl, f), jnp.float32),
            pltpu.SemaphoreType.DMA((16,)),
            pltpu.SemaphoreType.DMA((2,)),
            pltpu.SemaphoreType.DMA((2,)),
            pltpu.SemaphoreType.DMA((2,)),
            pltpu.SemaphoreType.DMA((2, 5)),
            pltpu.SemaphoreType.DMA((2, 5)),
            pltpu.SemaphoreType.DMA((2,)),
            pltpu.SemaphoreType.DMA((2,)),
            pltpu.SemaphoreType.DMA((2,)),
            pltpu.SemaphoreType.DMA((2,)),
        ],
        compiler_params=pltpu.CompilerParams(
            collective_id=0, has_side_effects=True, vmem_limit_bytes=62 * 1024 * 1024
        ),
        cost_estimate=pl.CostEstimate(
            flops=2_500_000_000, bytes_accessed=8_000_000, transcendentals=0
        ),
        name="section",
    )(coarse, up_weight, up_bias, mix_weight, mix_bias)


def solution(mesh):
    placed = (
        P("tile", None, None, "filt"),
        P("filt", None),
        P("filt"),
        P(None, "filt", None),
        P("filt"),
    )
    return jax.shard_map(
        local, mesh=mesh, in_specs=placed, out_specs=P("tile", None, None, "filt"), check_vma=False
    )
```
